512 devices in a mesh: seq: 64 (over z, y_lo, core), tp: 8 (over x, y_hi).
Axes of the slice: x: 4, y: 4 (y_hi: 2, y_lo: 2; y = y_hi * 2 + y_lo), z: 16, core: 2. Of those that a mesh axis runs over, the one named last changes fastest.
Arguments:
- query: bfloat16 [8192, 2048], P('seq', 'tp'), may hold values from -5 to 5
- key: bfloat16 [8192, 2048], P('seq', 'tp'), may hold values from -5 to 5
- value: bfloat16 [8192, 2048], P('seq', 'tp'), may hold values from -6 to 6
- documents: int32 [64], P('seq'), may hold values from 1 to 64, as said below
- frames: int32 [64], P('seq'), may hold values 0 or 1
- out_cotangent: bfloat16 [8192, 4096], P(('seq', 'tp')), may hold values from -6 to 6
- output_weight: bfloat16 [2048, 4096], P('tp'), may hold values from -0.125 to 0.125
Outputs:
- attended: bfloat16 [8192, 2048], P('seq', 'tp')
- query_grads: bfloat16 [8192, 2048], P('seq', 'tp')
- key_grads: bfloat16 [8192, 2048], P('seq', 'tp')
- value_grads: bfloat16 [8192, 2048], P('seq', 'tp')
The draws below stay inside these ranges and needn't reach their ends.
Inputs may be any that keep to these rules, and one draw needn't show every extreme that they name: documents never falls along the window; a tile's id is one plus the index of its document's first tile; a new document begins at the first tile of each aligned stretch of 2048 tokens and at the last tile of the window.
All inputs are finite; a program needn't handle non-finite values. No bound on the sum of `frames` on one device may be relied on, other than what follows from the above.
Results may differ from the reference program's by a relative error of at most 0.035.
Values may be sent and summed in bfloat16 or wider, within the bound.
A program may use at most 64 MiB of HBM per device.

```python
import jax
import jax.numpy as jnp
from jax import lax

D = 4096
HEAD_DIM = 128
H = 16
TILE = 128
STRETCH = 2048
TOKENS = 8192
TILES = 64


def draw_query(key, part):
    key = jax.random.fold_in(key, 1)
    values = jax.random.truncated_normal(key, -5.0, 5.0, (TOKENS, H * HEAD_DIM), jnp.float32)
    return values.astype(jnp.bfloat16)


def draw_key(key, part):
    key = jax.random.fold_in(key, 2)
    values = jax.random.truncated_normal(key, -5.0, 5.0, (TOKENS, H * HEAD_DIM), jnp.float32)
    return values.astype(jnp.bfloat16)


def draw_documents(key, part):
    key = jax.random.fold_in(key, 5)
    tile = jnp.arange(TILES, dtype=jnp.int32)
    starts = (jax.random.randint(key, (TILES,), 0, 6) == 0) | (tile % (STRETCH // TILE) == 0) | (tile == TILES - 1)
    marked = jnp.where(starts, tile + 1, 0).astype(jnp.int32)
    return lax.cummax(marked, axis=0).astype(jnp.int32)


def with_ends(entries, rng, least, top_value):
    spot = [jax.random.randint(jax.random.fold_in(rng, axis), (), 0, length) for axis, length in enumerate(entries.shape)]
    main_axis = entries.shape.index(max(entries.shape))
    next_to = spot[:main_axis] + [(spot[main_axis] + 1) % entries.shape[main_axis]] + spot[main_axis + 1:]
    return entries.at[tuple(spot)].set(least).at[tuple(next_to)].set(top_value)


def shard_levels(rng, shape, cuts, low, largest):
    factor_of, own = 1.0, jax.random.fold_in(rng, 6)
    for position, blocks in cuts:
        draws = jnp.exp(jax.random.uniform(jax.random.fold_in(own, position), (blocks,), jnp.float32, low / len(cuts), largest / len(cuts)))
        factor_of = factor_of * jnp.repeat(draws, shape[position] // blocks).reshape([-1 if axis == position else 1 for axis in range(len(shape))])
    return factor_of


def centred(rng, dims, deviation, most, pieces=(), held_as=jnp.bfloat16):
    gain = shard_levels(rng, dims, pieces, -0.22, 0.18) if pieces else 1.0
    drawn = jax.random.normal(rng, dims, jnp.float32) * deviation * gain
    return jnp.minimum(jnp.maximum(drawn, -most), most).astype(held_as)


def setup_inputs(seed: int = 0) -> dict:
    streams_of = jax.random.split(jax.random.key(seed), 8)
    return {
        "query": draw_query(jax.random.fold_in(streams_of[7], 71), 0),
        "key": draw_key(jax.random.fold_in(streams_of[7], 71), 0),
        "value": centred(streams_of[2], (TOKENS, H * HEAD_DIM), 1.0, 6.0, ((0, 64), (1, 8))),
        "documents": draw_documents(jax.random.fold_in(streams_of[7], 71), 0),
        "frames": with_ends((jax.random.randint(streams_of[4], (TILES,), 0, 2) < 1).astype(jnp.int32), jax.random.fold_in(streams_of[4], 1), 0, 1),
        "out_cotangent": centred(streams_of[5], (TOKENS, D), 1.0, 6.0, ((0, 512),)),
        "output_weight": centred(streams_of[6], (H * HEAD_DIM, D), (H * HEAD_DIM) ** -0.5, 0.125, ((0, 8),)),
    }


far_below = -1.0e30


def token_level(tiles):
    return jnp.broadcast_to(tiles[:, None], (tiles.shape[0], TILE)).reshape(-1)


def rounded(values):
    return lax.optimization_barrier(values.astype(jnp.bfloat16)).astype(jnp.float32)


def matmul(left, right):
    return jnp.dot(left, right, precision=lax.Precision.HIGHEST, preferred_element_type=jnp.float32)


def visible_pairs(query_place, query_document, query_frame, key_place, key_document):
    same_document = query_document[:, None] == key_document[None, :]
    earlier = key_place[None, :] <= query_place[:, None]
    same_tile = (query_place[:, None] // TILE) == (key_place[None, :] // TILE)
    return same_document & (earlier | (same_tile & (query_frame[:, None] == 1)))


def one_head(items):
    query, key, value, cotangent, document, frame = items
    place = jnp.arange(STRETCH, dtype=jnp.int32)
    mask = visible_pairs(place, document, frame, place, document)
    query_f = query.astype(jnp.float32)
    key_f = key.astype(jnp.float32)
    value_f = value.astype(jnp.float32)
    cotangent_f = cotangent.astype(jnp.float32)
    scores = jnp.where(mask, matmul(query_f, key_f.T) * HEAD_DIM ** -0.5, far_below)
    top = jnp.max(scores, axis=1)
    weights = jnp.where(mask, jnp.exp(scores - top[:, None]), 0.0)
    total = jnp.sum(weights, axis=1)
    log_total = top + jnp.log(total)
    attended = (matmul(rounded(weights), value_f) / total[:, None]).astype(jnp.bfloat16)
    delta = jnp.sum(cotangent_f * attended.astype(jnp.float32), axis=1)
    chances = jnp.where(mask, jnp.exp(scores - log_total[:, None]), 0.0)
    pushes = matmul(cotangent_f, value_f.T)
    slopes = rounded(HEAD_DIM ** -0.5 * chances * (pushes - delta[:, None]))
    query_grads = matmul(slopes, key_f).astype(jnp.bfloat16)
    key_grads = matmul(slopes.T, query_f).astype(jnp.bfloat16)
    value_grads = matmul(rounded(chances).T, cotangent_f).astype(jnp.bfloat16)
    return attended, query_grads, key_grads, value_grads


def reference(query, key, value, documents, frames, out_cotangent, output_weight):
    count = TOKENS // STRETCH

    def per_head(rows_in):
        return rows_in.reshape(count, STRETCH, H, HEAD_DIM).transpose(0, 2, 1, 3).reshape(count * H, STRETCH, HEAD_DIM)

    def back(heads):
        return heads.reshape(count, H, STRETCH, HEAD_DIM).transpose(0, 2, 1, 3).reshape(TOKENS, H * HEAD_DIM)

    cotangent = matmul(out_cotangent.astype(jnp.float32), output_weight.astype(jnp.float32).T).astype(jnp.bfloat16)
    document = jnp.repeat(token_level(documents).reshape(count, STRETCH), H, axis=0)
    frame = jnp.repeat(token_level(frames).reshape(count, STRETCH), H, axis=0)
    results = lax.map(one_head, (per_head(query), per_head(key), per_head(value), per_head(cotangent), document, frame))
    return back(results[0]), back(results[1]), back(results[2]), back(results[3])
```

```python
import functools

import jax
import jax.numpy as jnp
from jax import lax
from jax.experimental import pallas as pl
from jax.experimental.pallas import tpu as pltpu
from jax.sharding import PartitionSpec as P

MESH = pl.DeviceIdType.MESH
HEAD_DIM = 128
TILE = 128
SCALE = HEAD_DIM**-0.5
LOG2E = 1.4426950408889634
SCALE2 = SCALE * LOG2E
FAR_BELOW = -1.0e30
F32 = jnp.float32
BF16 = jnp.bfloat16


def nt(a, b):
    return lax.dot_general(a, b, (((1,), (1,)), ((), ())), preferred_element_type=F32)


def nn(a, b):
    return lax.dot_general(a, b, (((1,), (0,)), ((), ())), preferred_element_type=F32)


def kernel(
    q_hbm, k_hbm, v_hbm, doc_ref, frame_ref, x_hbm, w_hbm, out_ref,
    w, rows, kv_own, q_own, cot_own, kv, qb, cb, stats, stats_out, meta, scores,
    top, total, summed, dq, dk, dv, half_out, half_in, out_stage,
    load_sem, tp_send, tp_recv, kv_send, kv_pass, kv_recv, q_send, q_recv,
    c_send, c_recv, st_send, st_recv, meta_send, meta_recv, half_send, half_recv,
    out_send, out_recv,
):
    seq, tp = lax.axis_index("seq"), lax.axis_index("tp")
    plane = seq // 4
    first = (plane // 4) * 4
    z, y, c = plane % 4, (seq // 2) % 2, seq % 2
    x, hi = tp // 2, tp % 2
    far = 1 - hi

    def at(zz, yy, cc):
        return ((first + zz) * 4 + yy * 2 + cc, tp)

    def across(xx, hh):
        return (seq, ((xx + 4) % 4) * 2 + hh)

    def send(src, dst, send_sem, recv_sem, device):
        return pltpu.make_async_remote_copy(
            src_ref=src, dst_ref=dst, send_sem=send_sem, recv_sem=recv_sem,
            device_id=device, device_id_type=MESH,
        )

    mate = at(z, y, 1 - c)
    beside = at(z, 1 - y, c)
    x_up, x_down, x_far, y_far = across(x + 1, hi), across(x - 1, hi), across(x + 2, hi), across(x, far)

    barrier = pltpu.get_barrier_semaphore()
    for device in (x_up, x_down, x_far, y_far, mate):
        pl.semaphore_signal(barrier, inc=1, device_id=device, device_id_type=MESH)

    def greet(i, _):
        zz, yy = i // 2, i % 2

        @pl.when((zz != z) | (yy != y))
        def _():
            pl.semaphore_signal(barrier, inc=1, device_id=at(zz, yy, c), device_id_type=MESH)

        return 0

    lax.fori_loop(0, 8, greet, 0)

    def head(ref, h):
        return ref.at[:, pl.ds(h * HEAD_DIM, HEAD_DIM)]

    loads = [pltpu.make_async_copy(x_hbm, rows.at[hi, x], load_sem.at[0])]
    for h in range(2):
        loads.append(pltpu.make_async_copy(head(k_hbm, h), kv_own.at[h, 0], load_sem.at[1 + 3 * h]))
        loads.append(pltpu.make_async_copy(head(v_hbm, h), kv_own.at[h, 1], load_sem.at[2 + 3 * h]))
        loads.append(pltpu.make_async_copy(head(q_hbm, h), q_own.at[h], load_sem.at[3 + 3 * h]))
    load_w = pltpu.make_async_copy(w_hbm, w, load_sem.at[7])
    for load in loads:
        load.start()
    load_w.start()

    lane8 = lax.broadcasted_iota(jnp.int32, (8, 128), 0)
    begin = (doc_ref[0] - 1) * TILE - first * 512
    meta[y] = jnp.where(lane8 == 0, begin, frame_ref[0])

    for load in loads:
        load.wait()
    pl.semaphore_wait(barrier, 12)

    tp_first = [
        send(rows.at[hi, x], rows.at[hi, x], tp_send.at[i], tp_recv.at[i], device)
        for i, device in enumerate((x_up, x_down, x_far, y_far))
    ]
    for copy in tp_first:
        copy.start()

    def meta_copy():
        return send(meta.at[y], meta.at[y], meta_send, meta_recv, beside)

    def kv_copy(zz, h, device):
        return send(kv_own.at[h], kv.at[z, y, c], kv_send.at[zz, h], kv_recv.at[z, y, c], device)

    def q_copy(zz, h):
        return send(q_own.at[h], qb.at[z, y], q_send.at[zz, h], q_recv.at[z, y], at(zz, h, c))

    def c_copy(part, zz, h):
        return send(
            cot_own.at[h, :, part], cb.at[z, y, :, part], c_send.at[part, zz, h],
            c_recv.at[part, z, y], at(zz, h, c),
        )

    def all_kv(do):
        do(kv_copy(z, 1 - y, beside))
        do(kv_copy(z, y, mate))

        def step(zz, _):
            do(kv_copy(zz, y, at(zz, y, c)))
            do(kv_copy(zz, 1 - y, at(zz, 1 - y, c)))
            return 0

        lax.fori_loop(z + 1, 4, step, 0)

    def earlier(copy, do):
        do(copy(z, 1 - y))

        def step(i, _):
            zz = z - 1 - i
            do(copy(zz, y))
            do(copy(zz, 1 - y))
            return 0

        lax.fori_loop(0, z, step, 0)

    start = lambda copy: copy.start()
    sent = lambda copy: copy.wait_send()

    meta_copy().start()
    all_kv(start)
    earlier(q_copy, start)
    kv[z, y, c] = kv_own[y]
    qb[z, y] = q_own[y]

    def arrived_kv(zz, yy, cc):
        send(kv_own.at[0], kv.at[zz, yy, cc], kv_send.at[z, 0], kv_recv.at[zz, yy, cc], mate).wait_recv()

    def pass_kv(zz, yy):
        return send(kv.at[zz, yy, c], kv.at[zz, yy, c], kv_pass.at[zz, yy], kv_recv.at[zz, yy, c], mate)

    arrived_kv(z, 1 - y, c)
    pass_kv(z, 1 - y).start()

    tp_first[3].wait_recv()
    tp_second = [
        send(rows.at[far, x], rows.at[far, x], tp_send.at[4], tp_recv.at[4], x_up),
        send(rows.at[far, x], rows.at[far, x], tp_send.at[5], tp_recv.at[5], x_down),
    ]
    for copy in tp_second:
        copy.start()
    tp_first[2].wait_recv()
    x_other = (x + 2) % 4
    tp_second.append(
        send(rows.at[hi, x_other], rows.at[hi, x_other], tp_send.at[6], tp_recv.at[6], y_far)
    )
    tp_second[2].start()

    meta_copy().wait_recv()
    send(q_own.at[0], qb.at[z, y], q_send.at[z, 0], q_recv.at[z, 1 - y], mate).wait_recv()
    arrived_kv(z, y, 1 - c)
    arrived_kv(z, 1 - y, 1 - c)

    query = qb[z].reshape(256, HEAD_DIM)
    offset = lax.broadcasted_iota(jnp.int32, (128, 128), 0)
    low, high = [], []
    for tile in range(2):
        start_of = z * 512 + tile * 256 + c * 128
        low.append(jnp.broadcast_to(meta[tile][0:1], (128, 128)))
        framed = jnp.broadcast_to(meta[tile][1:2], (128, 128)) == 1
        high.append(jnp.where(framed, start_of + 127, start_of + offset))
    low = jnp.concatenate(low, axis=0)
    high = jnp.concatenate(high, axis=0)

    def keys_of(zz):
        return kv[zz, :, :, 0].reshape(512, HEAD_DIM)

    def values_of(zz):
        return kv[zz, :, :, 1].reshape(512, HEAD_DIM)

    def masked_scores(zz):
        place = zz * 512 + lax.broadcasted_iota(jnp.int32, (256, 512), 1)
        seen = (place >= low[:, :1]) & (place <= high[:, :1])
        return jnp.where(seen, nt(query, keys_of(zz)) * SCALE2, FAR_BELOW)

    s = masked_scores(z)
    scores[z] = s
    m = jnp.max(s, axis=1, keepdims=True)
    e = jnp.exp2(s - m)
    top[...] = jnp.broadcast_to(m, (256, 128))
    total[...] = jnp.broadcast_to(jnp.sum(e, axis=1, keepdims=True), (256, 128))
    summed[...] = nn(e.astype(BF16), values_of(z))

    def cotangent(part):
        block = nt(rows[part].reshape(64, -1), w[...]).astype(BF16)
        for h in range(2):
            cot_own[h, :, part] = block[:, h * 128 : (h + 1) * 128].reshape(4, 16, HEAD_DIM)
        cb[z, y, :, part] = cot_own[y, :, part]
        earlier(functools.partial(c_copy, part), start)

    tp_first[0].wait_recv()
    tp_first[1].wait_recv()
    load_w.wait()
    cotangent(hi)
    for copy in tp_second:
        copy.wait_recv()
    cotangent(far)

    def absorb(zz):
        s = masked_scores(zz)
        scores[zz] = s
        old = top[:, :1]
        m = jnp.maximum(old, jnp.max(s, axis=1, keepdims=True))
        e = jnp.exp2(s - m)
        factor = jnp.exp2(old - m)
        top[...] = jnp.broadcast_to(m, (256, 128))
        total[...] = total[...] * factor + jnp.sum(e, axis=1, keepdims=True)
        summed[...] = summed[...] * factor + nn(e.astype(BF16), values_of(zz))

    def forward_step(i, _):
        zz = z - 1 - i
        for yy in range(2):
            arrived_kv(zz, yy, c)
            pass_kv(zz, yy).start()
        for yy in range(2):
            arrived_kv(zz, yy, 1 - c)
        absorb(zz)
        return 0

    lax.fori_loop(0, z, forward_step, 0)

    attended = (summed[...] / total[...]).astype(BF16)
    log_total = top[...] + jnp.log2(total[...])

    def give(number, block):
        out_stage[number] = block.reshape(2, 128, HEAD_DIM)
        out_ref[number, y] = out_stage[number, y]
        out_copy(number).start()

    def out_copy(number):
        return send(
            out_stage.at[number, 1 - y], out_ref.at[number, y], out_send.at[number],
            out_recv.at[number], beside,
        )

    give(0, attended)

    def arrived_c(zz, yy):
        for part in range(2):
            send(
                cot_own.at[0, :, 0], cb.at[zz, yy, :, part], c_send.at[0, z, 0],
                c_recv.at[part, zz, yy], mate,
            ).wait_recv()

    arrived_c(z, 1 - y)
    own_cot = cb[z].reshape(256, HEAD_DIM)
    delta = jnp.sum(own_cot.astype(F32) * attended.astype(F32), axis=1, keepdims=True)
    lane = lax.broadcasted_iota(jnp.int32, (256, 128), 1)
    packed = jnp.where(
        lane == 0, log_total,
        jnp.where(lane == 1, delta, jnp.where(lane == 2, low.astype(F32), high.astype(F32))),
    )
    stats_out[...] = packed.T[:8]

    def st_copy(zz):
        return send(stats_out, stats.at[z], st_send.at[zz], st_recv.at[z], at(zz, y, c))

    def all_stats(do):
        def step(i, _):
            do(st_copy(z - 1 - i))
            return 0

        lax.fori_loop(0, z, step, 0)

    all_stats(start)
    stats[z] = stats_out[...]

    own_keys = keys_of(z)
    own_values = values_of(z)

    def key_side(zz):
        visit = qb[zz].reshape(256, HEAD_DIM)
        visit_cot = cb[zz].reshape(256, HEAD_DIM)
        rest = stats[zz]
        place = z * 512 + lax.broadcasted_iota(jnp.int32, (512, 256), 0)
        seen = (place >= rest[2:3].astype(jnp.int32)) & (place <= rest[3:4].astype(jnp.int32))
        s = jnp.where(seen, nt(own_keys, visit) * SCALE2, FAR_BELOW)
        p = jnp.exp2(s - rest[0:1])
        slopes = (p * (nt(own_values, visit_cot) - rest[1:2])).astype(BF16)
        return nn(slopes, visit), nn(p.astype(BF16), visit_cot)

    def query_side(zz):
        p = jnp.exp2(scores[zz] - log_total[:, :1])
        slopes = (p * (nt(own_cot, values_of(zz)) - delta)).astype(BF16)
        return nn(slopes, keys_of(zz))

    dk[...], dv[...] = key_side(z)
    dq[...] = query_side(z)

    def query_step(i, _):
        dq[...] += query_side(z - 1 - i)
        return 0

    lax.fori_loop(0, z, query_step, 0)
    give(1, (dq[...] * SCALE).astype(BF16))

    def key_step(zz, _):
        for yy in range(2):
            send(q_own.at[0], qb.at[zz, yy], q_send.at[z, 0], q_recv.at[zz, yy], mate).wait_recv()
            arrived_c(zz, yy)
        send(stats_out, stats.at[zz], st_send.at[z], st_recv.at[zz], mate).wait_recv()
        more_k, more_v = key_side(zz)
        dk[...] += more_k
        dv[...] += more_v
        return 0

    lax.fori_loop(z + 1, 4, key_step, 0)

    dk4 = dk.reshape(2, 2, 128, HEAD_DIM)
    dv4 = dv.reshape(2, 2, 128, HEAD_DIM)
    half_out[0] = dk4[:, 1 - c]
    half_out[1] = dv4[:, 1 - c]
    half = send(half_out, half_in, half_send, half_recv, mate)
    half.start()
    half.wait_recv()
    give(2, ((dk4[:, c] + half_in[0]) * SCALE).astype(BF16))
    give(3, (dv4[:, c] + half_in[1]).astype(BF16))

    for number in range(4):
        out_copy(number).wait_recv()

    for number in range(4):
        out_copy(number).wait_send()
    half.wait_send()
    for copy in tp_first + tp_second:
        copy.wait_send()
    meta_copy().wait_send()
    all_kv(sent)
    earlier(q_copy, sent)
    for part in range(2):
        earlier(functools.partial(c_copy, part), sent)
    all_stats(sent)
    pass_kv(z, 1 - y).wait_send()

    def passed(zz, _):
        for yy in range(2):
            pass_kv(zz, yy).wait_send()
        return 0

    lax.fori_loop(0, z, passed, 0)


def on_device(query, key, value, documents, frames, out_cotangent, output_weight):
    hbm = pl.BlockSpec(memory_space=pl.ANY)
    smem = pl.BlockSpec(memory_space=pltpu.SMEM)
    vmem = pltpu.VMEM
    dma = pltpu.SemaphoreType.DMA
    depth = out_cotangent.shape[1]
    out = pl.pallas_call(
        kernel,
        name="masked_attention",
        out_shape=jax.ShapeDtypeStruct((4, 2, 128, HEAD_DIM), BF16),
        in_specs=[hbm, hbm, hbm, smem, smem, hbm, hbm],
        out_specs=pl.BlockSpec(memory_space=vmem),
        scratch_shapes=[
            vmem((256, depth), BF16),
            vmem((2, 4, 16, depth), BF16),
            vmem((2, 2, 128, 128), BF16),
            vmem((2, 128, 128), BF16),
            vmem((2, 4, 2, 16, 128), BF16),
            vmem((4, 2, 2, 2, 128, 128), BF16),
            vmem((4, 2, 128, 128), BF16),
            vmem((4, 2, 4, 2, 16, 128), BF16),
            vmem((4, 8, 256), F32),
            vmem((8, 256), F32),
            vmem((2, 8, 128), jnp.int32),
            vmem((4, 256, 512), F32),
            vmem((256, 128), F32),
            vmem((256, 128), F32),
            vmem((256, 128), F32),
            vmem((256, 128), F32),
            vmem((512, 128), F32),
            vmem((512, 128), F32),
            vmem((2, 2, 128, 128), F32),
            vmem((2, 2, 128, 128), F32),
            vmem((4, 2, 128, 128), BF16),
            dma((8,)),
            dma((7,)), dma((7,)),
            dma((4, 2)), dma((4, 2)), dma((4, 2, 2)),
            dma((4, 2)), dma((4, 2)),
            dma((2, 4, 2)), dma((2, 4, 2)),
            dma((4,)), dma((4,)),
            dma, dma,
            dma, dma,
            dma((4,)), dma((4,)),
        ],
        compiler_params=pltpu.CompilerParams(
            collective_id=0, has_side_effects=True, vmem_limit_bytes=48 * 2**20
        ),
    )(query, key, value, documents, frames, out_cotangent, output_weight)
    return tuple(out[i].transpose(1, 0, 2).reshape(128, 256) for i in range(4))


def solution(mesh):
    whole = P("seq", "tp")
    return jax.shard_map(
        on_device,
        mesh=mesh,
        in_specs=(whole, whole, whole, P("seq"), P("seq"), P(("seq", "tp"), None), P("tp", None)),
        out_specs=(whole, whole, whole, whole),
        check_vma=False,
    )
```

```python
import contextlib
import functools

import jax
import jax.numpy as jnp
from jax import lax
from jax.experimental import pallas as pl
from jax.experimental.pallas import tpu as pltpu
from jax.sharding import PartitionSpec as P

MESH = pl.DeviceIdType.MESH
HEAD_DIM = 128
TILE = 128
SCALE = HEAD_DIM**-0.5
LOG2E = 1.4426950408889634
SCALE2 = SCALE * LOG2E
FAR_BELOW = -1.0e30
F32 = jnp.float32
BF16 = jnp.bfloat16
SCOPES = False


def scope(name):
    return jax.named_scope(name) if SCOPES else contextlib.nullcontext()


def nt(a, b):
    return lax.dot_general(a, b, (((1,), (1,)), ((), ())), preferred_element_type=F32)


def nn(a, b):
    return lax.dot_general(a, b, (((1,), (0,)), ((), ())), preferred_element_type=F32)


def kernel(
    q_hbm, k_hbm, v_hbm, doc_hbm, frame_hbm, x_hbm, w_hbm, out_ref,
    w, rows, kv_own, q_own, cot_own, kv, qb, cb, stats, stats_out, meta, scores,
    visits, top, total, summed, dq, dk, dv, half_out, half_in, out_stage,
    doc_ref, frame_ref, load_sem, tp_send, tp_recv, kv_send, kv_pass, kv_recv, q_send, q_recv,
    c_send, c_recv, st_send, st_recv, meta_send, meta_recv, half_send, half_recv,
    out_send, out_recv,
):
    seq, tp = lax.axis_index("seq"), lax.axis_index("tp")
    plane = seq // 4
    first = (plane // 4) * 4
    z, y, c = plane % 4, (seq // 2) % 2, seq % 2
    x, hi = tp // 2, tp % 2
    far = 1 - hi

    def at(zz, yy, cc):
        return ((first + zz) * 4 + yy * 2 + cc, tp)

    def across(xx, hh):
        return (seq, ((xx + 4) % 4) * 2 + hh)

    def send(src, dst, send_sem, recv_sem, device):
        return pltpu.make_async_remote_copy(
            src_ref=src, dst_ref=dst, send_sem=send_sem, recv_sem=recv_sem,
            device_id=device, device_id_type=MESH,
        )

    mate = at(z, y, 1 - c)
    beside = at(z, 1 - y, c)
    x_up, x_down, x_far, y_far = across(x + 1, hi), across(x - 1, hi), across(x + 2, hi), (
        at(z, 1 - y, c)[0], x * 2 + far
    )

    barrier = pltpu.get_barrier_semaphore()
    for device in (x_up, x_down, x_far, y_far, mate):
        pl.semaphore_signal(barrier, inc=1, device_id=device, device_id_type=MESH)

    def greet(i, _):
        zz, yy = i // 2, i % 2

        @pl.when((zz != z) | (yy != y))
        def _():
            pl.semaphore_signal(barrier, inc=1, device_id=at(zz, yy, c), device_id_type=MESH)

        return 0

    lax.fori_loop(0, 8, greet, 0)

    def head(ref, h):
        return ref.at[:, pl.ds(h * HEAD_DIM, HEAD_DIM)]

    loads = [pltpu.make_async_copy(x_hbm, rows.at[hi, x], load_sem.at[0])]
    for h in range(2):
        loads.append(pltpu.make_async_copy(head(k_hbm, h), kv_own.at[h, 0], load_sem.at[1 + 3 * h]))
        loads.append(pltpu.make_async_copy(head(v_hbm, h), kv_own.at[h, 1], load_sem.at[2 + 3 * h]))
        loads.append(pltpu.make_async_copy(head(q_hbm, h), q_own.at[h], load_sem.at[3 + 3 * h]))
    load_w = pltpu.make_async_copy(w_hbm, w, load_sem.at[7])
    for load in loads:
        load.start()
    load_w.start()
    marks = [
        pltpu.make_async_copy(doc_hbm, doc_ref, load_sem.at[8]),
        pltpu.make_async_copy(frame_hbm, frame_ref, load_sem.at[9]),
    ]
    for load in marks:
        load.start()
    for load in marks:
        load.wait()

    lane8 = lax.broadcasted_iota(jnp.int32, (8, 128), 0)
    begin = (doc_ref[0] - 1) * TILE - first * 512
    meta[y] = jnp.where(lane8 == 0, begin, frame_ref[0])

    with scope("load"):
        for load in loads:
            load.wait()
    with scope("barrier"):
        pl.semaphore_wait(barrier, 12)

    tp_first = [
        send(rows.at[hi, x], rows.at[hi, x], tp_send.at[i], tp_recv.at[i], device)
        for i, device in enumerate((x_up, x_down, x_far, y_far))
    ]
    with scope("tp_start"):
        for i in (3, 2, 0, 1):
            tp_first[i].start()

    def meta_copy():
        return send(meta.at[y], meta.at[y], meta_send, meta_recv, beside)

    def kv_copy(zz, h, device):
        return send(kv_own.at[h], kv.at[z, y, c], kv_send.at[zz, h], kv_recv.at[z, y, c], device)

    def q_copy(zz, h):
        return send(q_own.at[h], qb.at[z, y], q_send.at[zz, h], q_recv.at[z, y], at(zz, h, c))

    near_pair = pl.ds((x // 2) * 2, 2)
    far_pair = pl.ds(2 - (x // 2) * 2, 2)

    def part_of(ref, part):
        if part == 0:
            return ref.at[:, hi]
        return ref.at[near_pair if part == 1 else far_pair, far]

    def tile_of(part):
        return y if part == 0 else 1 - y

    def c_copy(part, zz, h):
        return send(
            part_of(cot_own.at[h], part), part_of(cb.at[z, tile_of(part)], part),
            c_send.at[part, zz, h], c_recv.at[part, z, tile_of(part)], at(zz, h, c),
        )

    def arrived_c(part, zz, yy):
        send(
            part_of(cot_own.at[0], part), part_of(cb.at[zz, yy], part), c_send.at[0, z, 0],
            c_recv.at[part, zz, yy], mate,
        ).wait_recv()

    def all_kv(do):
        do(kv_copy(z, 1 - y, beside))
        do(kv_copy(z, y, mate))

        def step(zz, _):
            do(kv_copy(zz, y, at(zz, y, c)))
            do(kv_copy(zz, 1 - y, at(zz, 1 - y, c)))
            return 0

        lax.fori_loop(z + 1, 4, step, 0)

    def earlier(copy, do):
        do(copy(z, 1 - y))
        below(copy, do)

    def below(copy, do):
        def step(i, _):
            do(copy(i, y))
            do(copy(i, 1 - y))
            return 0

        lax.fori_loop(0, z, step, 0)

    start = lambda copy: copy.start()
    sent = lambda copy: copy.wait_send()

    with scope("kvq_start"):
        meta_copy().start()
        all_kv(start)
        q_copy(z, 1 - y).start()
        kv[z, y, c] = kv_own[y]
        qb[z, y] = q_own[y]

    def arrived_kv(zz, yy, cc):
        send(kv_own.at[0], kv.at[zz, yy, cc], kv_send.at[z, 0], kv_recv.at[zz, yy, cc], mate).wait_recv()

    def pass_kv(zz, yy):
        return send(kv.at[zz, yy, c], kv.at[zz, yy, c], kv_pass.at[zz, yy], kv_recv.at[zz, yy, c], mate)

    with scope("kv_beside"):
        arrived_kv(z, 1 - y, c)
        pass_kv(z, 1 - y).start()

    with scope("tp_yfar"):
        tp_first[3].wait_recv()
    tp_second = [
        send(rows.at[far, x], rows.at[far, x], tp_send.at[4], tp_recv.at[4], x_up),
        send(rows.at[far, x], rows.at[far, x], tp_send.at[5], tp_recv.at[5], x_down),
    ]
    for copy in tp_second:
        copy.start()
    with scope("tp_xfar"):
        tp_first[2].wait_recv()
    x_other = (x + 2) % 4
    tp_second.append(
        send(rows.at[hi, x_other], rows.at[hi, x_other], tp_send.at[6], tp_recv.at[6], y_far)
    )
    tp_second[2].start()
    below(q_copy, start)

    with scope("own_group_wait"):
        meta_copy().wait_recv()
        send(q_own.at[0], qb.at[z, y], q_send.at[z, 0], q_recv.at[z, 1 - y], mate).wait_recv()
        arrived_kv(z, y, 1 - c)
        arrived_kv(z, 1 - y, 1 - c)

    query = qb[z].reshape(256, HEAD_DIM)
    offset = lax.broadcasted_iota(jnp.int32, (128, 128), 0)
    low, high = [], []
    for tile in range(2):
        start_of = z * 512 + tile * 256 + c * 128
        low.append(jnp.broadcast_to(meta[tile][0:1], (128, 128)))
        framed = jnp.broadcast_to(meta[tile][1:2], (128, 128)) == 1
        high.append(jnp.where(framed, start_of + 127, start_of + offset))
    low = jnp.concatenate(low, axis=0)
    high = jnp.concatenate(high, axis=0)

    def keys_of(zz):
        return kv[zz, :, :, 0].reshape(512, HEAD_DIM)

    def values_of(zz):
        return kv[zz, :, :, 1].reshape(512, HEAD_DIM)

    def masked_scores(zz):
        place = zz * 512 + lax.broadcasted_iota(jnp.int32, (256, 512), 1)
        seen = (place >= low[:, :1]) & (place <= high[:, :1])
        return jnp.where(seen, nt(query, keys_of(zz)) * SCALE2, FAR_BELOW)

    with scope("fwd_own_group"):
        s = masked_scores(z)
        scores[z] = s
        m = jnp.max(s, axis=1, keepdims=True)
        e = jnp.exp2(s - m)
        top[...] = jnp.broadcast_to(m, (256, 128))
        total[...] = jnp.broadcast_to(jnp.sum(e, axis=1, keepdims=True), (256, 128))
        summed[...] = nn(e.astype(BF16), values_of(z))

    def cotangent(part):
        if part == 0:
            picked, count = rows[hi], 4
        else:
            picked, count = rows[far, near_pair if part == 1 else far_pair], 2
        block = nt(picked.reshape(count * 16, -1), w[...]).astype(BF16)
        for h in range(2):
            mine = block[:, h * 128 : (h + 1) * 128].reshape(count, 16, HEAD_DIM)
            if part == 0:
                cot_own[h, :, hi] = mine
            else:
                cot_own[h, near_pair if part == 1 else far_pair, far] = mine
        if part == 0:
            cb[z, y, :, hi] = cot_own[y, :, hi]
        else:
            pair = near_pair if part == 1 else far_pair
            cb[z, 1 - y, pair, far] = cot_own[y, pair, far]
        earlier(functools.partial(c_copy, part), start)

    with scope("tp_near_wait"):
        tp_first[0].wait_recv()
        tp_first[1].wait_recv()
        load_w.wait()
    with scope("cot_near"):
        cotangent(0)

    def arrived_far(xx, number):
        send(rows.at[far, xx], rows.at[far, xx], tp_send.at[4], tp_recv.at[number], x_up).wait_recv()

    odd = x % 2
    with scope("tp_far_wait"):
        arrived_far(x + 1 - 2 * odd, 5 - odd)
    with scope("cot_far_1"):
        cotangent(1)
    with scope("tp_far_wait"):
        arrived_far((x + 3 + 2 * odd) % 4, 4 + odd)
        tp_second[2].wait_recv()
    with scope("cot_far_2"):
        cotangent(2)

    def absorb(zz):
        s = masked_scores(zz)
        scores[zz] = s
        old = top[:, :1]
        m = jnp.maximum(old, jnp.max(s, axis=1, keepdims=True))
        e = jnp.exp2(s - m)
        factor = jnp.exp2(old - m)
        top[...] = jnp.broadcast_to(m, (256, 128))
        total[...] = total[...] * factor + jnp.sum(e, axis=1, keepdims=True)
        summed[...] = summed[...] * factor + nn(e.astype(BF16), values_of(zz))

    def pass_step(i, _):
        zz = z - 1 - i
        with scope("kv_wait"):
            for yy in range(2):
                arrived_kv(zz, yy, c)
                pass_kv(zz, yy).start()
        return 0

    lax.fori_loop(0, z, pass_step, 0)

    def forward_step(i, _):
        zz = z - 1 - i
        with scope("absorb"):
            for yy in range(2):
                arrived_kv(zz, yy, 1 - c)
            absorb(zz)
        return 0

    lax.fori_loop(0, z, forward_step, 0)

    with scope("normalise"):
        attended = (summed[...] / total[...]).astype(BF16)
        log_total = top[...] + jnp.log2(total[...])

    def give(number, block):
        out_stage[number] = block.reshape(2, 128, HEAD_DIM)
        out_copy(number).start()
        out_keep(number).start()

    def out_keep(number):
        return pltpu.make_async_copy(
            out_stage.at[number, y], out_ref.at[number, y], load_sem.at[number]
        )

    def out_copy(number):
        return send(
            out_stage.at[number, 1 - y], out_ref.at[number, y], out_send.at[number],
            out_recv.at[number], beside,
        )

    give(0, attended)

    with scope("own_cot_wait"):
        arrived_c(0, z, 1 - y)
        arrived_c(1, z, y)
        arrived_c(2, z, y)
    with scope("delta"):
        own_cot = cb[z].reshape(256, HEAD_DIM)
        delta = jnp.sum(own_cot.astype(F32) * attended.astype(F32), axis=1, keepdims=True)
        lane = lax.broadcasted_iota(jnp.int32, (256, 128), 1)
        packed = jnp.where(
            lane == 0, log_total,
            jnp.where(lane == 1, delta, jnp.where(lane == 2, low.astype(F32), high.astype(F32))),
        )
        stats_out[...] = packed.T[:8]

    def st_copy(zz):
        return send(stats_out, stats.at[z], st_send.at[zz], st_recv.at[z], at(zz, y, c))

    def all_stats(do):
        def step(i, _):
            do(st_copy(z - 1 - i))
            return 0

        lax.fori_loop(0, z, step, 0)

    all_stats(start)
    stats[z] = stats_out[...]

    own_keys = keys_of(z)
    own_values = values_of(z)

    def key_side(zz):
        visit = qb[zz].reshape(256, HEAD_DIM)
        visit_cot = cb[zz].reshape(256, HEAD_DIM)
        rest = stats[zz]
        place = z * 512 + lax.broadcasted_iota(jnp.int32, (512, 256), 0)
        seen = (place >= rest[2:3].astype(jnp.int32)) & (place <= rest[3:4].astype(jnp.int32))
        s = jnp.where(seen, visits[zz] * SCALE2, FAR_BELOW)
        p = jnp.exp2(s - rest[0:1])
        slopes = (p * (nt(own_values, visit_cot) - rest[1:2])).astype(BF16)
        return nn(slopes, visit), nn(p.astype(BF16), visit_cot)

    def query_side(zz):
        p = jnp.exp2(scores[zz] - log_total[:, :1])
        slopes = (p * (nt(own_cot, values_of(zz)) - delta)).astype(BF16)
        return nn(slopes, keys_of(zz))

    visits[z] = nt(own_keys, query)
    with scope("key_side_own"):
        dk[...], dv[...] = key_side(z)
    with scope("query_side_own"):
        dq[...] = query_side(z)

    def query_step(i, _):
        with scope("query_side"):
            dq[...] += query_side(z - 1 - i)
        return 0

    lax.fori_loop(0, z, query_step, 0)
    give(1, (dq[...] * SCALE).astype(BF16))

    def arrived_q(zz, yy):
        send(q_own.at[0], qb.at[zz, yy], q_send.at[z, 0], q_recv.at[zz, yy], mate).wait_recv()

    def ahead(zz, _):
        arrived_q(zz, 0)
        arrived_q(zz, 1)
        visits[zz] = nt(own_keys, qb[zz].reshape(256, HEAD_DIM))
        return 0

    lax.fori_loop(z + 1, 4, ahead, 0)

    for copy in tp_first + tp_second:
        copy.wait_send()
    meta_copy().wait_send()
    all_kv(sent)
    earlier(q_copy, sent)
    for part in range(3):
        earlier(functools.partial(c_copy, part), sent)
    all_stats(sent)
    pass_kv(z, 1 - y).wait_send()

    def passed(zz, _):
        for yy in range(2):
            pass_kv(zz, yy).wait_send()
        return 0

    lax.fori_loop(0, z, passed, 0)

    def key_step(zz, _):
        with scope("qc_wait"):
            for yy in range(2):
                for part in range(3):
                    arrived_c(part, zz, yy)
        with scope("stats_wait"):
            send(stats_out, stats.at[zz], st_send.at[z], st_recv.at[zz], mate).wait_recv()
        with scope("key_side"):
            more_k, more_v = key_side(zz)
            dk[...] += more_k
            dv[...] += more_v
        return 0

    lax.fori_loop(z + 1, 4, key_step, 0)

    dk4 = dk.reshape(2, 2, 128, HEAD_DIM)
    dv4 = dv.reshape(2, 2, 128, HEAD_DIM)
    with scope("halves"):
        half_out[0] = dk4[:, 1 - c].astype(BF16)
        half_out[1] = dv4[:, 1 - c].astype(BF16)
        half = send(half_out, half_in, half_send, half_recv, mate)
        half.start()
        half.wait_recv()
    with scope("give_kv"):
        give(2, ((dk4[:, c] + half_in[0]) * SCALE).astype(BF16))
        give(3, (dv4[:, c] + half_in[1]).astype(BF16))

    with scope("out_wait"):
        for number in range(4):
            out_keep(number).wait()
            out_copy(number).wait_recv()

    for number in range(4):
        out_copy(number).wait_send()
    half.wait_send()


def spread_kernel(blocks, *refs):
    outs, sem = refs[:4], refs[4]
    copies = [
        pltpu.make_async_copy(
            blocks.at[i, h], outs[i].at[:, pl.ds(h * HEAD_DIM, HEAD_DIM)], sem.at[i, h]
        )
        for i in range(4)
        for h in range(2)
    ]
    for copy in copies:
        copy.start()
    for copy in copies:
        copy.wait()


def on_device(query, key, value, documents, frames, out_cotangent, output_weight):
    hbm = pl.BlockSpec(memory_space=pltpu.HBM)
    vmem = pltpu.VMEM
    dma = pltpu.SemaphoreType.DMA
    depth = out_cotangent.shape[1]
    out = pl.pallas_call(
        kernel,
        name="masked_attention",
        out_shape=pltpu.VMEM((4, 2, 128, HEAD_DIM), BF16),
        in_specs=[hbm] * 7,
        out_specs=pl.BlockSpec(memory_space=vmem),
        scratch_shapes=[
            vmem((256, depth), BF16),
            vmem((2, 4, 16, depth), BF16),
            vmem((2, 2, 128, 128), BF16),
            vmem((2, 128, 128), BF16),
            vmem((2, 4, 2, 16, 128), BF16),
            vmem((4, 2, 2, 2, 128, 128), BF16),
            vmem((4, 2, 128, 128), BF16),
            vmem((4, 2, 4, 2, 16, 128), BF16),
            vmem((4, 8, 256), F32),
            vmem((8, 256), F32),
            vmem((2, 8, 128), jnp.int32),
            vmem((4, 256, 512), F32),
            vmem((4, 512, 256), F32),
            vmem((256, 128), F32),
            vmem((256, 128), F32),
            vmem((256, 128), F32),
            vmem((256, 128), F32),
            vmem((512, 128), F32),
            vmem((512, 128), F32),
            vmem((2, 2, 128, 128), BF16),
            vmem((2, 2, 128, 128), BF16),
            vmem((4, 2, 128, 128), BF16),
            pltpu.SMEM((1,), jnp.int32), pltpu.SMEM((1,), jnp.int32),
            dma((10,)),
            dma((7,)), dma((7,)),
            dma((4, 2)), dma((4, 2)), dma((4, 2, 2)),
            dma((4, 2)), dma((4, 2)),
            dma((3, 4, 2)), dma((3, 4, 2)),
            dma((4,)), dma((4,)),
            dma, dma,
            dma, dma,
            dma((4,)), dma((4,)),
        ],
        compiler_params=pltpu.CompilerParams(
            collective_id=0, has_side_effects=True, vmem_limit_bytes=62 * 2**20
        ),
    )(query, key, value, documents, frames, out_cotangent, output_weight)
    return pl.pallas_call(
        spread_kernel,
        name="spread_heads",
        out_shape=[jax.ShapeDtypeStruct((128, 256), BF16)] * 4,
        in_specs=[pl.BlockSpec(memory_space=vmem)],
        out_specs=[hbm] * 4,
        scratch_shapes=[dma((4, 2))],
        compiler_params=pltpu.CompilerParams(vmem_limit_bytes=40 * 2**20),
    )(out)


def solution(mesh):
    whole = P("seq", "tp")
    return jax.shard_map(
        on_device,
        mesh=mesh,
        in_specs=(whole, whole, whole, P("seq"), P("seq"), P(("seq", "tp"), None), P("tp", None)),
        out_specs=(whole, whole, whole, whole),
        check_vma=False,
    )
```

```python
import contextlib
import functools

import jax
import jax.numpy as jnp
from jax import lax
from jax.experimental import pallas as pl
from jax.experimental.pallas import tpu as pltpu
from jax.sharding import PartitionSpec as P

MESH = pl.DeviceIdType.MESH
HEAD_DIM = 128
TILE = 128
SCALE = HEAD_DIM**-0.5
LOG2E = 1.4426950408889634
SCALE2 = SCALE * LOG2E
FAR_BELOW = -1.0e30
F32 = jnp.float32
BF16 = jnp.bfloat16
SCOPES = False


def scope(name):
    return jax.named_scope(name) if SCOPES else contextlib.nullcontext()


def nt(a, b):
    return lax.dot_general(a, b, (((1,), (1,)), ((), ())), preferred_element_type=F32)


def nn(a, b):
    return lax.dot_general(a, b, (((1,), (0,)), ((), ())), preferred_element_type=F32)


def kernel(
    q_hbm, k_hbm, v_hbm, doc_hbm, frame_hbm, x_hbm, w_hbm, out_ref,
    w, wt, rows, kv_own, q_own, cot_own, kv, qb, cb, stats, stats_out, meta, scores,
    visits, top, total, summed, dq, dk, dv, half_out, half_in, out_stage,
    doc_ref, frame_ref, load_sem, tp_send, tp_recv, kv_send, kv_pass, kv_relay, kv_recv, q_send, q_recv,
    c_send, c_recv, st_send, st_recv, meta_send, meta_recv, half_send, half_recv,
    out_send, out_recv,
):
    seq, tp = lax.axis_index("seq"), lax.axis_index("tp")
    plane = seq // 4
    first = (plane // 4) * 4
    z, y, c = plane % 4, (seq // 2) % 2, seq % 2
    x, hi = tp // 2, tp % 2
    far = 1 - hi

    def at(zz, yy, cc):
        return ((first + zz) * 4 + yy * 2 + cc, tp)

    def across(xx, hh):
        return (seq, ((xx + 4) % 4) * 2 + hh)

    def send(src, dst, send_sem, recv_sem, device):
        return pltpu.make_async_remote_copy(
            src_ref=src, dst_ref=dst, send_sem=send_sem, recv_sem=recv_sem,
            device_id=device, device_id_type=MESH,
        )

    mate = at(z, y, 1 - c)
    beside = at(z, 1 - y, c)
    x_up, x_down, x_far, y_far = across(x + 1, hi), across(x - 1, hi), across(x + 2, hi), (
        at(z, 1 - y, c)[0], x * 2 + far
    )

    barrier = pltpu.get_barrier_semaphore()
    for device in (x_up, x_down, x_far, y_far, mate):
        pl.semaphore_signal(barrier, inc=1, device_id=device, device_id_type=MESH)

    def greet(i, _):
        zz, yy = i // 2, i % 2

        @pl.when((zz != z) | (yy != y))
        def _():
            pl.semaphore_signal(barrier, inc=1, device_id=at(zz, yy, c), device_id_type=MESH)

        return 0

    lax.fori_loop(0, 8, greet, 0)

    def head(ref, h):
        return ref.at[:, pl.ds(h * HEAD_DIM, HEAD_DIM)]

    loads = [pltpu.make_async_copy(x_hbm, rows.at[hi, x], load_sem.at[0])]
    for h in range(2):
        loads.append(pltpu.make_async_copy(head(k_hbm, h), kv_own.at[h, 0], load_sem.at[1 + 3 * h]))
        loads.append(pltpu.make_async_copy(head(v_hbm, h), kv_own.at[h, 1], load_sem.at[2 + 3 * h]))
        loads.append(pltpu.make_async_copy(head(q_hbm, h), q_own.at[h], load_sem.at[3 + 3 * h]))
    load_w = pltpu.make_async_copy(w_hbm, w, load_sem.at[7])
    for load in loads:
        load.start()
    load_w.start()
    marks = [
        pltpu.make_async_copy(doc_hbm, doc_ref, load_sem.at[8]),
        pltpu.make_async_copy(frame_hbm, frame_ref, load_sem.at[9]),
    ]
    for load in marks:
        load.start()
    for load in marks:
        load.wait()

    lane8 = lax.broadcasted_iota(jnp.int32, (8, 128), 0)
    begin = (doc_ref[0] - 1) * TILE - first * 512
    meta[y] = jnp.where(lane8 == 0, begin, frame_ref[0])

    with scope("load"):
        for load in loads:
            load.wait()
    with scope("barrier"):
        pl.semaphore_wait(barrier, 12)

    tp_first = [
        send(rows.at[hi, x], rows.at[hi, x], tp_send.at[i], tp_recv.at[i], device)
        for i, device in enumerate((x_up, x_down, x_far, y_far))
    ]
    with scope("tp_start"):
        for i in (3, 2, 0, 1):
            tp_first[i].start()

    def meta_copy():
        return send(meta.at[y], meta.at[y], meta_send, meta_recv, beside)

    def kv_copy(zz, h, device):
        return send(kv_own.at[h], kv.at[z, y, c], kv_send.at[zz, h], kv_recv.at[z, y, c], device)

    def q_copy(zz, h):
        return send(q_own.at[h], qb.at[z, y], q_send.at[zz, h], q_recv.at[z, y], at(zz, h, c))

    def part_of(ref, part):
        return ref.at[:, hi if part == 0 else far]

    def tile_of(part):
        return y if part == 0 else 1 - y

    def c_copy(part, zz, h):
        return send(
            part_of(cot_own.at[h], part), part_of(cb.at[z, tile_of(part)], part),
            c_send.at[part, zz, h], c_recv.at[part, z, tile_of(part)], at(zz, h, c),
        )

    def arrived_c(part, zz, yy):
        send(
            part_of(cot_own.at[0], part), part_of(cb.at[zz, yy], part), c_send.at[0, z, 0],
            c_recv.at[part, zz, yy], mate,
        ).wait_recv()

    def all_kv(do):
        do(kv_copy(z, 1 - y, beside))
        do(kv_copy(z, y, mate))

        def step(zz, _):
            do(kv_copy(zz, y, at(zz, y, c)))
            do(kv_copy(zz, 1 - y, at(zz, 1 - y, c)))
            return 0

        lax.fori_loop(z + 1, 3 + (z + 3) // 4, step, 0)

    def earlier(copy, do):
        do(copy(z, 1 - y))
        below(copy, do)

    def below(copy, do):
        def step(i, _):
            do(copy(i, y))
            do(copy(i, 1 - y))
            return 0

        lax.fori_loop(0, z, step, 0)

    start = lambda copy: copy.start()
    sent = lambda copy: copy.wait_send()

    with scope("kvq_start"):
        meta_copy().start()
        all_kv(start)
        q_copy(z, 1 - y).start()
        below(q_copy, start)
        kv[z, y, c] = kv_own[y]
        qb[z, y] = q_own[y]

    def arrived_kv(zz, yy, cc):
        send(kv_own.at[0], kv.at[zz, yy, cc], kv_send.at[z, 0], kv_recv.at[zz, yy, cc], mate).wait_recv()

    def pass_kv(zz, yy):
        return send(kv.at[zz, yy, c], kv.at[zz, yy, c], kv_pass.at[zz, yy], kv_recv.at[zz, yy, c], mate)

    load_w.wait()

    def turn(i, _):
        here = pl.ds(pl.multiple_of(i * 256, 256), 256)
        wt[here, :] = w[:, here].T
        return 0

    lax.fori_loop(0, w.shape[1] // 256, turn, 0)

    with scope("tp_yfar"):
        tp_first[3].wait_recv()
    tp_second = [
        send(rows.at[far, x], rows.at[far, x], tp_send.at[4], tp_recv.at[4], x_up),
        send(rows.at[far, x], rows.at[far, x], tp_send.at[5], tp_recv.at[5], x_down),
    ]
    for copy in tp_second:
        copy.start()
    with scope("tp_xfar"):
        tp_first[2].wait_recv()
    x_other = (x + 2) % 4
    tp_second.append(
        send(rows.at[hi, x_other], rows.at[hi, x_other], tp_send.at[6], tp_recv.at[6], y_far)
    )
    tp_second[2].start()
    with scope("kv_beside"):
        arrived_kv(z, 1 - y, c)
        pass_kv(z, 1 - y).start()


    def relay(yy):
        return send(kv.at[0, yy, c], kv.at[0, yy, c], kv_relay.at[yy], kv_recv.at[0, yy, c], at(3, y, c))

    @pl.when(z == 2)
    def _():
        with scope("relay"):
            for yy in range(2):
                arrived_kv(0, yy, c)
                relay(yy).start()
                pass_kv(0, yy).start()

    with scope("own_group_wait"):
        meta_copy().wait_recv()
        send(q_own.at[0], qb.at[z, y], q_send.at[z, 0], q_recv.at[z, 1 - y], mate).wait_recv()
        arrived_kv(z, y, 1 - c)
        arrived_kv(z, 1 - y, 1 - c)

    query = qb[z].reshape(256, HEAD_DIM)
    offset = lax.broadcasted_iota(jnp.int32, (128, 128), 0)
    low, high = [], []
    for tile in range(2):
        start_of = z * 512 + tile * 256 + c * 128
        low.append(jnp.broadcast_to(meta[tile][0:1], (128, 128)))
        framed = jnp.broadcast_to(meta[tile][1:2], (128, 128)) == 1
        high.append(jnp.where(framed, start_of + 127, start_of + offset))
    low = jnp.concatenate(low, axis=0)
    high = jnp.concatenate(high, axis=0)

    def keys_of(zz):
        return kv[zz, :, :, 0].reshape(512, HEAD_DIM)

    def values_of(zz):
        return kv[zz, :, :, 1].reshape(512, HEAD_DIM)

    def masked_scores(zz):
        place = zz * 512 + lax.broadcasted_iota(jnp.int32, (256, 512), 1)
        seen = (place >= low[:, :1]) & (place <= high[:, :1])
        return jnp.where(seen, nt(query, keys_of(zz)) * SCALE2, FAR_BELOW)

    with scope("fwd_own_group"):
        s = masked_scores(z)
        scores[z] = s
        m = jnp.max(s, axis=1, keepdims=True)
        e = jnp.exp2(s - m)
        top[...] = jnp.broadcast_to(m, (256, 128))
        total[...] = jnp.broadcast_to(jnp.sum(e, axis=1, keepdims=True), (256, 128))
        summed[...] = nn(e.astype(BF16), values_of(z))

    def absorb(zz):
        s = masked_scores(zz)
        scores[zz] = s
        old = top[:, :1]
        m = jnp.maximum(old, jnp.max(s, axis=1, keepdims=True))
        e = jnp.exp2(s - m)
        factor = jnp.exp2(old - m)
        top[...] = jnp.broadcast_to(m, (256, 128))
        total[...] = total[...] * factor + jnp.sum(e, axis=1, keepdims=True)
        summed[...] = summed[...] * factor + nn(e.astype(BF16), values_of(zz))

    def take(zz):
        for yy in range(2):
            arrived_kv(zz, yy, c)
            pass_kv(zz, yy).start()

    def cotangent(part):
        half = hi if part == 0 else far
        block = nn(rows[half].reshape(64, -1), wt[...]).astype(BF16)
        for h in range(2):
            cot_own[h, :, half] = block[:, h * 128 : (h + 1) * 128].reshape(4, 16, HEAD_DIM)
        cb[z, tile_of(part), :, half] = cot_own[y, :, half]
        earlier(functools.partial(c_copy, part), start)

    with scope("tp_near_wait"):
        tp_first[0].wait_recv()
        tp_first[1].wait_recv()
    with scope("cot_near"):
        cotangent(0)

    @pl.when(z > 0)
    def _():
        with scope("kv_wait"):
            take(z - 1)

    @pl.when(z > 0)
    def _():
        with scope("absorb"):
            for yy in range(2):
                arrived_kv(z - 1, yy, 1 - c)
            absorb(z - 1)

    with scope("tp_far_wait"):
        for copy in tp_second:
            copy.wait_recv()
    with scope("cot_far"):
        cotangent(1)

    def take_step(i, _):
        zz = z - 1 - i
        with scope("kv_wait"):

            @pl.when(z != 2)
            def _():
                take(zz)

        return 0

    lax.fori_loop(1, z, take_step, 0)

    def forward_step(i, _):
        zz = z - 1 - i
        with scope("absorb"):
            for yy in range(2):
                arrived_kv(zz, yy, 1 - c)
            absorb(zz)
        return 0

    lax.fori_loop(1, z, forward_step, 0)

    with scope("normalise"):
        attended = (summed[...] / total[...]).astype(BF16)
        log_total = top[...] + jnp.log2(total[...])

    def give(number, block):
        out_stage[number] = block.reshape(2, 128, HEAD_DIM)
        out_copy(number).start()
        out_keep(number).start()

    def out_keep(number):
        return pltpu.make_async_copy(
            out_stage.at[number, y], out_ref.at[number, y], load_sem.at[number]
        )

    def out_copy(number):
        return send(
            out_stage.at[number, 1 - y], out_ref.at[number, y], out_send.at[number],
            out_recv.at[number], beside,
        )

    give(0, attended)

    with scope("own_cot_wait"):
        arrived_c(0, z, 1 - y)
        arrived_c(1, z, y)
    with scope("delta"):
        own_cot = cb[z].reshape(256, HEAD_DIM)
        delta = jnp.sum(own_cot.astype(F32) * attended.astype(F32), axis=1, keepdims=True)
        lane = lax.broadcasted_iota(jnp.int32, (256, 128), 1)
        packed = jnp.where(
            lane == 0, log_total,
            jnp.where(lane == 1, delta, jnp.where(lane == 2, low.astype(F32), high.astype(F32))),
        )
        stats_out[...] = packed.T[:8]

    def st_copy(zz):
        return send(stats_out, stats.at[z], st_send.at[zz], st_recv.at[z], at(zz, y, c))

    def all_stats(do):
        def step(i, _):
            do(st_copy(z - 1 - i))
            return 0

        lax.fori_loop(0, z, step, 0)

    all_stats(start)
    stats[z] = stats_out[...]

    own_keys = keys_of(z)
    own_values = values_of(z)

    def key_side(zz):
        visit = qb[zz].reshape(256, HEAD_DIM)
        visit_cot = cb[zz].reshape(256, HEAD_DIM)
        rest = stats[zz]
        place = z * 512 + lax.broadcasted_iota(jnp.int32, (512, 256), 0)
        seen = (place >= rest[2:3].astype(jnp.int32)) & (place <= rest[3:4].astype(jnp.int32))
        s = jnp.where(seen, visits[zz] * SCALE2, FAR_BELOW)
        p = jnp.exp2(s - rest[0:1])
        slopes = (p * (nt(own_values, visit_cot) - rest[1:2])).astype(BF16)
        return nn(slopes, visit), nn(p.astype(BF16), visit_cot)

    def query_side(zz):
        p = jnp.exp2(scores[zz] - log_total[:, :1])
        slopes = (p * (nt(own_cot, values_of(zz)) - delta)).astype(BF16)
        return nn(slopes, keys_of(zz))

    visits[z] = nt(own_keys, query)
    with scope("key_side_own"):
        dk[...], dv[...] = key_side(z)
    with scope("query_side_own"):
        dq[...] = query_side(z)

    def query_step(i, _):
        with scope("query_side"):
            dq[...] += query_side(z - 1 - i)
        return 0

    lax.fori_loop(0, z, query_step, 0)
    give(1, (dq[...] * SCALE).astype(BF16))

    def arrived_q(zz, yy):
        send(q_own.at[0], qb.at[zz, yy], q_send.at[z, 0], q_recv.at[zz, yy], mate).wait_recv()

    def ahead(zz, _):
        arrived_q(zz, 0)
        arrived_q(zz, 1)
        visits[zz] = nt(own_keys, qb[zz].reshape(256, HEAD_DIM))
        return 0

    lax.fori_loop(z + 1, 4, ahead, 0)

    for copy in tp_first + tp_second:
        copy.wait_send()
    meta_copy().wait_send()
    all_kv(sent)
    earlier(q_copy, sent)
    for part in range(2):
        earlier(functools.partial(c_copy, part), sent)
    all_stats(sent)
    pass_kv(z, 1 - y).wait_send()

    @pl.when(z == 2)
    def _():
        for yy in range(2):
            relay(yy).wait_send()

    def passed(zz, _):
        for yy in range(2):
            pass_kv(zz, yy).wait_send()
        return 0

    lax.fori_loop(0, z, passed, 0)

    def key_step(zz, _):
        with scope("qc_wait"):
            for yy in range(2):
                for part in range(2):
                    arrived_c(part, zz, yy)
        with scope("stats_wait"):
            send(stats_out, stats.at[zz], st_send.at[z], st_recv.at[zz], mate).wait_recv()
        with scope("key_side"):
            more_k, more_v = key_side(zz)
            dk[...] += more_k
            dv[...] += more_v
        return 0

    lax.fori_loop(z + 1, 4, key_step, 0)

    dk4 = dk.reshape(2, 2, 128, HEAD_DIM)
    dv4 = dv.reshape(2, 2, 128, HEAD_DIM)
    with scope("halves"):
        half_out[0] = dk4[:, 1 - c].astype(BF16)
        half_out[1] = dv4[:, 1 - c].astype(BF16)
        half = send(half_out, half_in, half_send, half_recv, mate)
        half.start()
        half.wait_recv()
    with scope("give_kv"):
        give(2, ((dk4[:, c] + half_in[0]) * SCALE).astype(BF16))
        give(3, (dv4[:, c] + half_in[1]).astype(BF16))

    with scope("out_wait"):
        for number in range(4):
            out_keep(number).wait()
            out_copy(number).wait_recv()

    for number in range(4):
        out_copy(number).wait_send()
    half.wait_send()


def spread_kernel(blocks, *refs):
    outs, sem = refs[:4], refs[4]
    copies = [
        pltpu.make_async_copy(
            blocks.at[i, h], outs[i].at[:, pl.ds(h * HEAD_DIM, HEAD_DIM)], sem.at[i, h]
        )
        for i in range(4)
        for h in range(2)
    ]
    for copy in copies:
        copy.start()
    for copy in copies:
        copy.wait()


def on_device(query, key, value, documents, frames, out_cotangent, output_weight):
    hbm = pl.BlockSpec(memory_space=pltpu.HBM)
    vmem = pltpu.VMEM
    dma = pltpu.SemaphoreType.DMA
    depth = out_cotangent.shape[1]
    out = pl.pallas_call(
        kernel,
        name="masked_attention",
        out_shape=pltpu.VMEM((4, 2, 128, HEAD_DIM), BF16),
        in_specs=[hbm] * 7,
        out_specs=pl.BlockSpec(memory_space=vmem),
        scratch_shapes=[
            vmem((256, depth), BF16),
            vmem((depth, 256), BF16),
            vmem((2, 4, 16, depth), BF16),
            vmem((2, 2, 128, 128), BF16),
            vmem((2, 128, 128), BF16),
            vmem((2, 4, 2, 16, 128), BF16),
            vmem((4, 2, 2, 2, 128, 128), BF16),
            vmem((4, 2, 128, 128), BF16),
            vmem((4, 2, 4, 2, 16, 128), BF16),
            vmem((4, 8, 256), F32),
            vmem((8, 256), F32),
            vmem((2, 8, 128), jnp.int32),
            vmem((4, 256, 512), F32),
            vmem((4, 512, 256), F32),
            vmem((256, 128), F32),
            vmem((256, 128), F32),
            vmem((256, 128), F32),
            vmem((256, 128), F32),
            vmem((512, 128), F32),
            vmem((512, 128), F32),
            vmem((2, 2, 128, 128), BF16),
            vmem((2, 2, 128, 128), BF16),
            vmem((4, 2, 128, 128), BF16),
            pltpu.SMEM((1,), jnp.int32), pltpu.SMEM((1,), jnp.int32),
            dma((10,)),
            dma((7,)), dma((7,)),
            dma((4, 2)), dma((4, 2)), dma((2,)), dma((4, 2, 2)),
            dma((4, 2)), dma((4, 2)),
            dma((2, 4, 2)), dma((2, 4, 2)),
            dma((4,)), dma((4,)),
            dma, dma,
            dma, dma,
            dma((4,)), dma((4,)),
        ],
        compiler_params=pltpu.CompilerParams(
            collective_id=0, has_side_effects=True, vmem_limit_bytes=62 * 2**20
        ),
    )(query, key, value, documents, frames, out_cotangent, output_weight)
    return pl.pallas_call(
        spread_kernel,
        name="spread_heads",
        out_shape=[jax.ShapeDtypeStruct((128, 256), BF16)] * 4,
        in_specs=[pl.BlockSpec(memory_space=vmem)],
        out_specs=[hbm] * 4,
        scratch_shapes=[dma((4, 2))],
        compiler_params=pltpu.CompilerParams(vmem_limit_bytes=40 * 2**20),
    )(out)


def solution(mesh):
    whole = P("seq", "tp")
    return jax.shard_map(
        on_device,
        mesh=mesh,
        in_specs=(whole, whole, whole, P("seq"), P("seq"), P(("seq", "tp"), None), P("tp", None)),
        out_specs=(whole, whole, whole, whole),
        check_vma=False,
    )
```

```python
import contextlib
import functools

import jax
import jax.numpy as jnp
from jax import lax
from jax.experimental import pallas as pl
from jax.experimental.pallas import tpu as pltpu
from jax.sharding import PartitionSpec as P

MESH = pl.DeviceIdType.MESH
HEAD_DIM = 128
TILE = 128
SCALE = HEAD_DIM**-0.5
LOG2E = 1.4426950408889634
SCALE2 = SCALE * LOG2E
FAR_BELOW = -1.0e30
F32 = jnp.float32
BF16 = jnp.bfloat16
SCOPES = False


def scope(name):
    return jax.named_scope(name) if SCOPES else contextlib.nullcontext()


def nt(a, b):
    return lax.dot_general(a, b, (((1,), (1,)), ((), ())), preferred_element_type=F32)


def nn(a, b):
    return lax.dot_general(a, b, (((1,), (0,)), ((), ())), preferred_element_type=F32)


def kernel(
    q_hbm, k_hbm, v_hbm, doc_hbm, frame_hbm, x_hbm, w_hbm, out_ref,
    w, wt, rows, kv_own, q_own, cot_own, kv, qb, cb, stats, stats_out, meta, scores,
    visits, top, total, summed, dq, dk, dv, shares, got, out_stage,
    doc_ref, frame_ref, load_sem, tp_send, tp_recv, kv_send, kv_pass, kv_relay, kv_recv, q_send, q_recv,
    c_send, c_recv, st_send, st_recv, meta_send, meta_recv, share_send, share_recv,
    out_send, out_recv,
):
    seq, tp = lax.axis_index("seq"), lax.axis_index("tp")
    plane = seq // 4
    first = (plane // 4) * 4
    z, y, c = plane % 4, (seq // 2) % 2, seq % 2
    x, hi = tp // 2, tp % 2
    far = 1 - hi

    def at(zz, yy, cc):
        return ((first + zz) * 4 + yy * 2 + cc, tp)

    def across(xx, hh):
        return (seq, ((xx + 4) % 4) * 2 + hh)

    def send(src, dst, send_sem, recv_sem, device):
        return pltpu.make_async_remote_copy(
            src_ref=src, dst_ref=dst, send_sem=send_sem, recv_sem=recv_sem,
            device_id=device, device_id_type=MESH,
        )

    mate = at(z, y, 1 - c)
    beside = at(z, 1 - y, c)
    x_up, x_down, x_far, y_far = across(x + 1, hi), across(x - 1, hi), across(x + 2, hi), (
        at(z, 1 - y, c)[0], x * 2 + far
    )

    barrier = pltpu.get_barrier_semaphore()
    for device in (x_up, x_down, x_far, y_far, mate, at(z, 1 - y, 1 - c)):
        pl.semaphore_signal(barrier, inc=1, device_id=device, device_id_type=MESH)

    def greet(i, _):
        zz, yy = i // 2, i % 2

        @pl.when((zz != z) | (yy != y))
        def _():
            pl.semaphore_signal(barrier, inc=1, device_id=at(zz, yy, c), device_id_type=MESH)

        return 0

    lax.fori_loop(0, 8, greet, 0)

    def head(ref, h):
        return ref.at[:, pl.ds(h * HEAD_DIM, HEAD_DIM)]

    loads = [pltpu.make_async_copy(x_hbm, rows.at[hi, x], load_sem.at[0])]
    for h in range(2):
        loads.append(pltpu.make_async_copy(head(k_hbm, h), kv_own.at[h, 0], load_sem.at[1 + 3 * h]))
        loads.append(pltpu.make_async_copy(head(v_hbm, h), kv_own.at[h, 1], load_sem.at[2 + 3 * h]))
        loads.append(pltpu.make_async_copy(head(q_hbm, h), q_own.at[h], load_sem.at[3 + 3 * h]))
    load_w = pltpu.make_async_copy(w_hbm, w, load_sem.at[7])
    for load in loads:
        load.start()
    load_w.start()
    marks = [
        pltpu.make_async_copy(doc_hbm, doc_ref, load_sem.at[8]),
        pltpu.make_async_copy(frame_hbm, frame_ref, load_sem.at[9]),
    ]
    for load in marks:
        load.start()
    for load in marks:
        load.wait()

    lane8 = lax.broadcasted_iota(jnp.int32, (8, 128), 0)
    begin = (doc_ref[0] - 1) * TILE - first * 512
    meta[y] = jnp.where(lane8 == 0, begin, frame_ref[0])

    with scope("load"):
        for load in loads:
            load.wait()
    with scope("barrier"):
        pl.semaphore_wait(barrier, 13)

    tp_first = [
        send(rows.at[hi, x], rows.at[hi, x], tp_send.at[i], tp_recv.at[i], device)
        for i, device in enumerate((x_up, x_down, x_far, y_far))
    ]
    with scope("tp_start"):
        for i in (3, 2, 0, 1):
            tp_first[i].start()

    def meta_copy():
        return send(meta.at[y], meta.at[y], meta_send, meta_recv, beside)

    def kv_copy(zz, h, device):
        return send(kv_own.at[h], kv.at[z, y, c], kv_send.at[zz, h], kv_recv.at[z, y, c], device)

    def q_copy(zz, h):
        return send(q_own.at[h], qb.at[z, y], q_send.at[zz, h], q_recv.at[z, y], at(zz, h, c))

    def part_of(ref, part):
        return ref.at[:, hi if part == 0 else far]

    def tile_of(part):
        return y if part == 0 else 1 - y

    def c_copy(part, zz, h):
        return send(
            part_of(cot_own.at[h], part), part_of(cb.at[z, tile_of(part)], part),
            c_send.at[part, zz, h], c_recv.at[part, z, tile_of(part)], at(zz, h, c),
        )

    def arrived_c(part, zz, yy):
        send(
            part_of(cot_own.at[0], part), part_of(cb.at[zz, yy], part), c_send.at[0, z, 0],
            c_recv.at[part, zz, yy], mate,
        ).wait_recv()

    def all_kv(do):
        do(kv_copy(z, 1 - y, beside))
        do(kv_copy(z, y, mate))

        def step(zz, _):
            do(kv_copy(zz, y, at(zz, y, c)))
            do(kv_copy(zz, 1 - y, at(zz, 1 - y, c)))
            return 0

        lax.fori_loop(z + 1, 3 + (z + 3) // 4, step, 0)

    def earlier(copy, do):
        do(copy(z, 1 - y))
        below(copy, do)

    def below(copy, do):
        def step(i, _):
            do(copy(i, y))
            do(copy(i, 1 - y))
            return 0

        lax.fori_loop(0, z, step, 0)

    start = lambda copy: copy.start()
    sent = lambda copy: copy.wait_send()

    with scope("kvq_start"):
        meta_copy().start()
        all_kv(start)
        q_copy(z, 1 - y).start()
        below(q_copy, start)
        kv[z, y, c] = kv_own[y]
        qb[z, y] = q_own[y]

    def arrived_kv(zz, yy, cc):
        send(kv_own.at[0], kv.at[zz, yy, cc], kv_send.at[z, 0], kv_recv.at[zz, yy, cc], mate).wait_recv()

    def pass_kv(zz, yy):
        return send(kv.at[zz, yy, c], kv.at[zz, yy, c], kv_pass.at[zz, yy], kv_recv.at[zz, yy, c], mate)

    load_w.wait()

    def turn(i, _):
        here = pl.ds(pl.multiple_of(i * 256, 256), 256)
        wt[here, :] = w[:, here].T
        return 0

    lax.fori_loop(0, w.shape[1] // 256, turn, 0)

    with scope("tp_yfar"):
        tp_first[3].wait_recv()
    tp_second = [
        send(rows.at[far, x], rows.at[far, x], tp_send.at[4], tp_recv.at[4], x_up),
        send(rows.at[far, x], rows.at[far, x], tp_send.at[5], tp_recv.at[5], x_down),
    ]
    for copy in tp_second:
        copy.start()
    with scope("tp_xfar"):
        tp_first[2].wait_recv()
    x_other = (x + 2) % 4
    tp_second.append(
        send(rows.at[hi, x_other], rows.at[hi, x_other], tp_send.at[6], tp_recv.at[6], y_far)
    )
    tp_second[2].start()
    with scope("kv_beside"):
        arrived_kv(z, 1 - y, c)
        pass_kv(z, 1 - y).start()


    def relay(yy):
        return send(kv.at[0, yy, c], kv.at[0, yy, c], kv_relay.at[yy], kv_recv.at[0, yy, c], at(3, y, c))

    @pl.when(z == 2)
    def _():
        with scope("relay"):
            for yy in range(2):
                arrived_kv(0, yy, c)
                relay(yy).start()
                pass_kv(0, yy).start()

    with scope("own_group_wait"):
        meta_copy().wait_recv()
        send(q_own.at[0], qb.at[z, y], q_send.at[z, 0], q_recv.at[z, 1 - y], mate).wait_recv()
        arrived_kv(z, y, 1 - c)
        arrived_kv(z, 1 - y, 1 - c)

    query = qb[z].reshape(256, HEAD_DIM)
    offset = lax.broadcasted_iota(jnp.int32, (128, 128), 0)
    low, high = [], []
    for tile in range(2):
        start_of = z * 512 + tile * 256 + c * 128
        low.append(jnp.broadcast_to(meta[tile][0:1], (128, 128)))
        framed = jnp.broadcast_to(meta[tile][1:2], (128, 128)) == 1
        high.append(jnp.where(framed, start_of + 127, start_of + offset))
    low = jnp.concatenate(low, axis=0)
    high = jnp.concatenate(high, axis=0)

    def keys_of(zz):
        return kv[zz, :, :, 0].reshape(512, HEAD_DIM)

    def values_of(zz):
        return kv[zz, :, :, 1].reshape(512, HEAD_DIM)

    def masked_scores(zz):
        place = zz * 512 + lax.broadcasted_iota(jnp.int32, (256, 512), 1)
        seen = (place >= low[:, :1]) & (place <= high[:, :1])
        return jnp.where(seen, nt(query, keys_of(zz)) * SCALE2, FAR_BELOW)

    with scope("fwd_own_group"):
        s = masked_scores(z)
        scores[z] = s
        m = jnp.max(s, axis=1, keepdims=True)
        e = jnp.exp2(s - m)
        top[...] = jnp.broadcast_to(m, (256, 128))
        total[...] = jnp.broadcast_to(jnp.sum(e, axis=1, keepdims=True), (256, 128))
        summed[...] = nn(e.astype(BF16), values_of(z))

    def absorb(zz):
        s = masked_scores(zz)
        scores[zz] = s
        old = top[:, :1]
        m = jnp.maximum(old, jnp.max(s, axis=1, keepdims=True))
        e = jnp.exp2(s - m)
        factor = jnp.exp2(old - m)
        top[...] = jnp.broadcast_to(m, (256, 128))
        total[...] = total[...] * factor + jnp.sum(e, axis=1, keepdims=True)
        summed[...] = summed[...] * factor + nn(e.astype(BF16), values_of(zz))

    def take(zz):
        for yy in range(2):
            arrived_kv(zz, yy, c)
            pass_kv(zz, yy).start()

    def cotangent(part):
        half = hi if part == 0 else far
        block = nn(rows[half].reshape(64, -1), wt[...]).astype(BF16)
        for h in range(2):
            cot_own[h, :, half] = block[:, h * 128 : (h + 1) * 128].reshape(4, 16, HEAD_DIM)
        cb[z, tile_of(part), :, half] = cot_own[y, :, half]
        earlier(functools.partial(c_copy, part), start)

    with scope("tp_near_wait"):
        tp_first[0].wait_recv()
        tp_first[1].wait_recv()
    with scope("cot_near"):
        cotangent(0)

    @pl.when(z > 0)
    def _():
        with scope("kv_wait"):
            take(z - 1)

    @pl.when(z > 0)
    def _():
        with scope("absorb"):
            for yy in range(2):
                arrived_kv(z - 1, yy, 1 - c)
            absorb(z - 1)

    with scope("tp_far_wait"):
        for copy in tp_second:
            copy.wait_recv()
    with scope("cot_far"):
        cotangent(1)

    def take_step(i, _):
        zz = z - 1 - i
        with scope("kv_wait"):

            @pl.when(z != 2)
            def _():
                take(zz)

        return 0

    lax.fori_loop(1, z, take_step, 0)

    def forward_step(i, _):
        zz = z - 1 - i
        with scope("absorb"):
            for yy in range(2):
                arrived_kv(zz, yy, 1 - c)
            absorb(zz)
        return 0

    lax.fori_loop(1, z, forward_step, 0)

    with scope("normalise"):
        attended = (summed[...] / total[...]).astype(BF16)
        log_total = top[...] + jnp.log2(total[...])

    def give(number, block):
        out_stage[number] = block.reshape(2, 128, HEAD_DIM)
        out_copy(number).start()
        out_keep(number).start()

    def out_keep(number):
        return pltpu.make_async_copy(
            out_stage.at[number, y], out_ref.at[number, y], load_sem.at[number]
        )

    def out_copy(number):
        return send(
            out_stage.at[number, 1 - y], out_ref.at[number, y], out_send.at[number],
            out_recv.at[number], beside,
        )

    give(0, attended)

    with scope("own_cot_wait"):
        arrived_c(0, z, 1 - y)
        arrived_c(1, z, y)
    with scope("delta"):
        own_cot = cb[z].reshape(256, HEAD_DIM)
        delta = jnp.sum(own_cot.astype(F32) * attended.astype(F32), axis=1, keepdims=True)
        lane = lax.broadcasted_iota(jnp.int32, (256, 128), 1)
        packed = jnp.where(
            lane == 0, log_total,
            jnp.where(lane == 1, delta, jnp.where(lane == 2, low.astype(F32), high.astype(F32))),
        )
        stats_out[...] = packed.T[:8]

    def st_copy(zz):
        return send(stats_out, stats.at[z], st_send.at[zz], st_recv.at[z], at(zz, y, c))

    def all_stats(do):
        def step(i, _):
            do(st_copy(z - 1 - i))
            return 0

        lax.fori_loop(0, z, step, 0)

    all_stats(start)
    stats[z] = stats_out[...]

    own_keys = keys_of(z)
    own_values = values_of(z)

    def key_side(zz):
        visit = qb[zz].reshape(256, HEAD_DIM)
        visit_cot = cb[zz].reshape(256, HEAD_DIM)
        rest = stats[zz]
        place = z * 512 + lax.broadcasted_iota(jnp.int32, (512, 256), 0)
        seen = (place >= rest[2:3].astype(jnp.int32)) & (place <= rest[3:4].astype(jnp.int32))
        s = jnp.where(seen, visits[zz], FAR_BELOW)
        p = jnp.exp2(s - rest[0:1])
        slopes = (p * (nt(own_values, visit_cot) - rest[1:2])).astype(BF16)
        return nn(slopes, visit), nn(p.astype(BF16), visit_cot)

    def query_side(zz):
        p = jnp.exp2(scores[zz] - log_total[:, :1])
        slopes = (p * (nt(own_cot, values_of(zz)) - delta)).astype(BF16)
        return nn(slopes, keys_of(zz))

    visits[z] = nt(own_keys, query) * SCALE2
    with scope("key_side_own"):
        dk[...], dv[...] = key_side(z)
    with scope("query_side_own"):
        dq[...] = query_side(z)

    def query_step(i, _):
        with scope("query_side"):
            dq[...] += query_side(z - 1 - i)
        return 0

    lax.fori_loop(0, z, query_step, 0)
    give(1, (dq[...] * SCALE).astype(BF16))

    def arrived_q(zz, yy):
        send(q_own.at[0], qb.at[zz, yy], q_send.at[z, 0], q_recv.at[zz, yy], mate).wait_recv()

    def ahead(zz, _):
        arrived_q(zz, 0)
        arrived_q(zz, 1)
        visits[zz] = nt(own_keys, qb[zz].reshape(256, HEAD_DIM)) * SCALE2
        return 0

    lax.fori_loop(z + 1, 4, ahead, 0)

    for copy in tp_first + tp_second:
        copy.wait_send()
    meta_copy().wait_send()
    all_kv(sent)
    earlier(q_copy, sent)
    for part in range(2):
        earlier(functools.partial(c_copy, part), sent)
    all_stats(sent)
    pass_kv(z, 1 - y).wait_send()

    @pl.when(z == 2)
    def _():
        for yy in range(2):
            relay(yy).wait_send()

    def passed(zz, _):
        for yy in range(2):
            pass_kv(zz, yy).wait_send()
        return 0

    lax.fori_loop(0, z, passed, 0)

    def key_step(zz, _):
        with scope("qc_wait"):
            for yy in range(2):
                for part in range(2):
                    arrived_c(part, zz, yy)
        with scope("stats_wait"):
            send(stats_out, stats.at[zz], st_send.at[z], st_recv.at[zz], mate).wait_recv()
        with scope("key_side"):
            more_k, more_v = key_side(zz)
            dk[...] += more_k
            dv[...] += more_v
        return 0

    lax.fori_loop(z + 1, 4, key_step, 0)

    owners = [(1 - y, c), (1 - y, 1 - c), (y, 1 - c)]

    def share_copy(number):
        yy, cc = owners[number]
        return send(
            shares.at[yy, cc], got.at[y, c], share_send.at[number], share_recv.at[y, c],
            at(z, yy, cc),
        )

    with scope("shares"):
        for number, (yy, cc) in enumerate(owners + [(y, c)]):
            keys = pl.ds(pl.multiple_of((2 * yy + cc) * 128, 128), 128)
            shares[yy, cc, 0] = (dk[keys, :] * SCALE).astype(BF16)
            shares[yy, cc, 1] = dv[keys, :].astype(BF16)
            if number < 3:
                share_copy(number).start()
        got[y, c] = shares[y, c]
    with scope("shares_wait"):
        for yy, cc in owners:
            send(
                shares.at[0, 0], got.at[yy, cc], share_send.at[0], share_recv.at[yy, cc], mate
            ).wait_recv()
        for kind in range(2):
            for h in range(2):
                both = got[h, 0, kind].astype(F32) + got[h, 1, kind].astype(F32)
                out_ref[2 + kind, h] = both.astype(BF16)

    with scope("out_wait"):
        for number in range(2):
            out_keep(number).wait()
            out_copy(number).wait_recv()

    for number in range(2):
        out_copy(number).wait_send()
    for number in range(3):
        share_copy(number).wait_send()


def spread_kernel(blocks, *refs):
    outs, sem = refs[:4], refs[4]
    copies = [
        pltpu.make_async_copy(
            blocks.at[i, h], outs[i].at[:, pl.ds(h * HEAD_DIM, HEAD_DIM)], sem.at[i, h]
        )
        for i in range(4)
        for h in range(2)
    ]
    for copy in copies:
        copy.start()
    for copy in copies:
        copy.wait()


def on_device(query, key, value, documents, frames, out_cotangent, output_weight):
    hbm = pl.BlockSpec(memory_space=pltpu.HBM)
    vmem = pltpu.VMEM
    dma = pltpu.SemaphoreType.DMA
    depth = out_cotangent.shape[1]
    out = pl.pallas_call(
        kernel,
        name="masked_attention",
        out_shape=pltpu.VMEM((4, 2, 128, HEAD_DIM), BF16),
        in_specs=[hbm] * 7,
        out_specs=pl.BlockSpec(memory_space=vmem),
        scratch_shapes=[
            vmem((256, depth), BF16),
            vmem((depth, 256), BF16),
            vmem((2, 4, 16, depth), BF16),
            vmem((2, 2, 128, 128), BF16),
            vmem((2, 128, 128), BF16),
            vmem((2, 4, 2, 16, 128), BF16),
            vmem((4, 2, 2, 2, 128, 128), BF16),
            vmem((4, 2, 128, 128), BF16),
            vmem((4, 2, 4, 2, 16, 128), BF16),
            vmem((4, 8, 256), F32),
            vmem((8, 256), F32),
            vmem((2, 8, 128), jnp.int32),
            vmem((4, 256, 512), F32),
            vmem((4, 512, 256), F32),
            vmem((256, 128), F32),
            vmem((256, 128), F32),
            vmem((256, 128), F32),
            vmem((256, 128), F32),
            vmem((512, 128), F32),
            vmem((512, 128), F32),
            vmem((2, 2, 2, 128, 128), BF16),
            vmem((2, 2, 2, 128, 128), BF16),
            vmem((4, 2, 128, 128), BF16),
            pltpu.SMEM((1,), jnp.int32), pltpu.SMEM((1,), jnp.int32),
            dma((10,)),
            dma((7,)), dma((7,)),
            dma((4, 2)), dma((4, 2)), dma((2,)), dma((4, 2, 2)),
            dma((4, 2)), dma((4, 2)),
            dma((2, 4, 2)), dma((2, 4, 2)),
            dma((4,)), dma((4,)),
            dma, dma,
            dma((3,)), dma((2, 2)),
            dma((4,)), dma((4,)),
        ],
        compiler_params=pltpu.CompilerParams(
            collective_id=0, has_side_effects=True, vmem_limit_bytes=62 * 2**20
        ),
    )(query, key, value, documents, frames, out_cotangent, output_weight)
    return pl.pallas_call(
        spread_kernel,
        name="spread_heads",
        out_shape=[jax.ShapeDtypeStruct((128, 256), BF16)] * 4,
        in_specs=[pl.BlockSpec(memory_space=vmem)],
        out_specs=[hbm] * 4,
        scratch_shapes=[dma((4, 2))],
        compiler_params=pltpu.CompilerParams(vmem_limit_bytes=40 * 2**20),
    )(out)


def solution(mesh):
    whole = P("seq", "tp")
    return jax.shard_map(
        on_device,
        mesh=mesh,
        in_specs=(whole, whole, whole, P("seq"), P("seq"), P(("seq", "tp"), None), P("tp", None)),
        out_specs=(whole, whole, whole, whole),
        check_vma=False,
    )
```

```python
import contextlib
import functools

import jax
import jax.numpy as jnp
from jax import lax
from jax.experimental import pallas as pl
from jax.experimental.pallas import tpu as pltpu
from jax.sharding import PartitionSpec as P

MESH = pl.DeviceIdType.MESH
HEAD_DIM = 128
TILE = 128
SCALE = HEAD_DIM**-0.5
LOG2E = 1.4426950408889634
SCALE2 = SCALE * LOG2E
FAR_BELOW = -1.0e30
F32 = jnp.float32
BF16 = jnp.bfloat16
SCOPES = False


def scope(name):
    return jax.named_scope(name) if SCOPES else contextlib.nullcontext()


def nt(a, b):
    return lax.dot_general(a, b, (((1,), (1,)), ((), ())), preferred_element_type=F32)


def nn(a, b):
    return lax.dot_general(a, b, (((1,), (0,)), ((), ())), preferred_element_type=F32)


def kernel(
    q_hbm, k_hbm, v_hbm, doc_hbm, frame_hbm, x_hbm, w_hbm, out_ref,
    w, wt, rows, kv_own, q_own, cot_own, kv, qb, cb, stats, stats_out, meta, scores,
    visits, top, total, summed, dq, dk, dv, half_out, half_in, out_stage,
    doc_ref, frame_ref, load_sem, tp_send, tp_recv, kv_send, kv_pass, kv_relay, kv_recv, q_send, q_recv,
    c_send, c_recv, st_send, st_recv, meta_send, meta_recv, half_send, half_recv,
    out_send, out_recv,
):
    seq, tp = lax.axis_index("seq"), lax.axis_index("tp")
    plane = seq // 4
    first = (plane // 4) * 4
    z, y, c = plane % 4, (seq // 2) % 2, seq % 2
    x, hi = tp // 2, tp % 2
    far = 1 - hi

    def at(zz, yy, cc):
        return ((first + zz) * 4 + yy * 2 + cc, tp)

    def across(xx, hh):
        return (seq, ((xx + 4) % 4) * 2 + hh)

    def send(src, dst, send_sem, recv_sem, device):
        return pltpu.make_async_remote_copy(
            src_ref=src, dst_ref=dst, send_sem=send_sem, recv_sem=recv_sem,
            device_id=device, device_id_type=MESH,
        )

    mate = at(z, y, 1 - c)
    beside = at(z, 1 - y, c)
    x_up, x_down, x_far, y_far = across(x + 1, hi), across(x - 1, hi), across(x + 2, hi), (
        at(z, 1 - y, c)[0], x * 2 + far
    )

    barrier = pltpu.get_barrier_semaphore()
    def greet(i, _):
        zz, yy = i // 2, i % 2

        @pl.when((zz != z) | (yy != y))
        def _():
            pl.semaphore_signal(barrier, inc=1, device_id=at(zz, yy, c), device_id_type=MESH)

        return 0

    lax.fori_loop(0, 8, greet, 0)
    for device in (x_up, x_down, x_far, y_far, mate):
        pl.semaphore_signal(barrier, inc=1, device_id=device, device_id_type=MESH)

    def head(ref, h):
        return ref.at[:, pl.ds(h * HEAD_DIM, HEAD_DIM)]

    loads = [pltpu.make_async_copy(x_hbm, rows.at[hi, x], load_sem.at[0])]
    for h in range(2):
        loads.append(pltpu.make_async_copy(head(k_hbm, h), kv_own.at[h, 0], load_sem.at[1 + 3 * h]))
        loads.append(pltpu.make_async_copy(head(v_hbm, h), kv_own.at[h, 1], load_sem.at[2 + 3 * h]))
        loads.append(pltpu.make_async_copy(head(q_hbm, h), q_own.at[h], load_sem.at[3 + 3 * h]))
    load_w = pltpu.make_async_copy(w_hbm, w, load_sem.at[7])
    for load in loads:
        load.start()
    load_w.start()
    marks = [
        pltpu.make_async_copy(doc_hbm, doc_ref, load_sem.at[8]),
        pltpu.make_async_copy(frame_hbm, frame_ref, load_sem.at[9]),
    ]
    for load in marks:
        load.start()
    for load in marks:
        load.wait()

    lane8 = lax.broadcasted_iota(jnp.int32, (8, 128), 0)
    begin = (doc_ref[0] - 1) * TILE - first * 512
    meta[y] = jnp.where(lane8 == 0, begin, frame_ref[0])

    with scope("load"):
        for load in loads:
            load.wait()
    with scope("barrier"):
        pl.semaphore_wait(barrier, 12)

    tp_first = [
        send(rows.at[hi, x], rows.at[hi, x], tp_send.at[i], tp_recv.at[i], device)
        for i, device in enumerate((x_up, x_down, x_far, y_far))
    ]
    with scope("tp_start"):
        for i in (3, 2, 0, 1):
            tp_first[i].start()

    def meta_copy():
        return send(meta.at[y], meta.at[y], meta_send, meta_recv, beside)

    def kv_copy(zz, h, device):
        return send(kv_own.at[h], kv.at[z, y, c], kv_send.at[zz, h], kv_recv.at[z, y, c], device)

    def q_copy(zz, h):
        return send(q_own.at[h], qb.at[z, y], q_send.at[zz, h], q_recv.at[z, y], at(zz, h, c))

    def part_of(ref, part):
        return ref.at[:, hi if part == 0 else far]

    def tile_of(part):
        return y if part == 0 else 1 - y

    def c_copy(part, zz, h):
        return send(
            part_of(cot_own.at[h], part), part_of(cb.at[z, tile_of(part)], part),
            c_send.at[part, zz, h], c_recv.at[part, z, tile_of(part)], at(zz, h, c),
        )

    def arrived_c(part, zz, yy):
        send(
            part_of(cot_own.at[0], part), part_of(cb.at[zz, yy], part), c_send.at[0, z, 0],
            c_recv.at[part, zz, yy], mate,
        ).wait_recv()

    def all_kv(do):
        do(kv_copy(z, 1 - y, beside))
        do(kv_copy(z, y, mate))

        def step(zz, _):
            do(kv_copy(zz, y, at(zz, y, c)))
            do(kv_copy(zz, 1 - y, at(zz, 1 - y, c)))
            return 0

        lax.fori_loop(z + 1, 3 + (z + 3) // 4, step, 0)

    def earlier(copy, do):
        do(copy(z, 1 - y))
        below(copy, do)

    def below(copy, do):
        def step(i, _):
            do(copy(i, y))
            do(copy(i, 1 - y))
            return 0

        lax.fori_loop(0, z, step, 0)

    start = lambda copy: copy.start()
    sent = lambda copy: copy.wait_send()

    with scope("kvq_start"):
        meta_copy().start()
        all_kv(start)
        q_copy(z, 1 - y).start()
        below(q_copy, start)
        kv[z, y, c] = kv_own[y]
        qb[z, y] = q_own[y]

    def arrived_kv(zz, yy, cc):
        send(kv_own.at[0], kv.at[zz, yy, cc], kv_send.at[z, 0], kv_recv.at[zz, yy, cc], mate).wait_recv()

    def pass_kv(zz, yy):
        return send(kv.at[zz, yy, c], kv.at[zz, yy, c], kv_pass.at[zz, yy], kv_recv.at[zz, yy, c], mate)

    load_w.wait()

    def turn(i, _):
        here = pl.ds(pl.multiple_of(i * 256, 256), 256)
        wt[here, :] = w[:, here].T
        return 0

    lax.fori_loop(0, w.shape[1] // 256, turn, 0)

    with scope("tp_yfar"):
        tp_first[3].wait_recv()
    tp_second = [
        send(rows.at[far, x], rows.at[far, x], tp_send.at[4], tp_recv.at[4], x_up),
        send(rows.at[far, x], rows.at[far, x], tp_send.at[5], tp_recv.at[5], x_down),
    ]
    for copy in tp_second:
        copy.start()
    with scope("tp_xfar"):
        tp_first[2].wait_recv()
    x_other = (x + 2) % 4
    tp_second.append(
        send(rows.at[hi, x_other], rows.at[hi, x_other], tp_send.at[6], tp_recv.at[6], y_far)
    )
    tp_second[2].start()
    with scope("kv_beside"):
        arrived_kv(z, 1 - y, c)
        pass_kv(z, 1 - y).start()


    def relay(yy):
        return send(kv.at[0, yy, c], kv.at[0, yy, c], kv_relay.at[yy], kv_recv.at[0, yy, c], at(3, y, c))

    @pl.when(z == 2)
    def _():
        with scope("relay"):
            for yy in range(2):
                arrived_kv(0, yy, c)
                relay(yy).start()
                pass_kv(0, yy).start()

    with scope("own_group_wait"):
        meta_copy().wait_recv()
        send(q_own.at[0], qb.at[z, y], q_send.at[z, 0], q_recv.at[z, 1 - y], mate).wait_recv()
        arrived_kv(z, y, 1 - c)
        arrived_kv(z, 1 - y, 1 - c)

    query = qb[z].reshape(256, HEAD_DIM)
    offset = lax.broadcasted_iota(jnp.int32, (128, 128), 0)
    low, high = [], []
    for tile in range(2):
        start_of = z * 512 + tile * 256 + c * 128
        low.append(jnp.broadcast_to(meta[tile][0:1], (128, 128)))
        framed = jnp.broadcast_to(meta[tile][1:2], (128, 128)) == 1
        high.append(jnp.where(framed, start_of + 127, start_of + offset))
    low = jnp.concatenate(low, axis=0)
    high = jnp.concatenate(high, axis=0)

    def keys_of(zz):
        return kv[zz, :, :, 0].reshape(512, HEAD_DIM)

    def values_of(zz):
        return kv[zz, :, :, 1].reshape(512, HEAD_DIM)

    def masked_scores(zz):
        place = zz * 512 + lax.broadcasted_iota(jnp.int32, (256, 512), 1)
        seen = (place >= low[:, :1]) & (place <= high[:, :1])
        return jnp.where(seen, nt(query, keys_of(zz)) * SCALE2, FAR_BELOW)

    with scope("fwd_own_group"):
        s = masked_scores(z)
        scores[z] = s
        m = jnp.max(s, axis=1, keepdims=True)
        e = jnp.exp2(s - m)
        top[...] = jnp.broadcast_to(m, (256, 128))
        total[...] = jnp.broadcast_to(jnp.sum(e, axis=1, keepdims=True), (256, 128))
        summed[...] = nn(e.astype(BF16), values_of(z))

    def absorb(zz):
        s = masked_scores(zz)
        scores[zz] = s
        old = top[:, :1]
        m = jnp.maximum(old, jnp.max(s, axis=1, keepdims=True))
        e = jnp.exp2(s - m)
        factor = jnp.exp2(old - m)
        top[...] = jnp.broadcast_to(m, (256, 128))
        total[...] = total[...] * factor + jnp.sum(e, axis=1, keepdims=True)
        summed[...] = summed[...] * factor + nn(e.astype(BF16), values_of(zz))

    def take(zz):
        for yy in range(2):
            arrived_kv(zz, yy, c)
            pass_kv(zz, yy).start()

    def cotangent(part):
        half = hi if part == 0 else far
        block = nn(rows[half].reshape(64, -1), wt[...]).astype(BF16)
        for h in range(2):
            cot_own[h, :, half] = block[:, h * 128 : (h + 1) * 128].reshape(4, 16, HEAD_DIM)
        cb[z, tile_of(part), :, half] = cot_own[y, :, half]
        earlier(functools.partial(c_copy, part), start)

    with scope("tp_near_wait"):
        tp_first[0].wait_recv()
        tp_first[1].wait_recv()
    with scope("cot_near"):
        cotangent(0)

    @pl.when(z > 0)
    def _():
        with scope("kv_wait"):
            take(z - 1)

    @pl.when(z > 0)
    def _():
        with scope("absorb"):
            for yy in range(2):
                arrived_kv(z - 1, yy, 1 - c)
            absorb(z - 1)

    with scope("tp_far_wait"):
        for copy in tp_second:
            copy.wait_recv()
    with scope("cot_far"):
        cotangent(1)

    def take_step(i, _):
        zz = z - 1 - i
        with scope("kv_wait"):

            @pl.when(z != 2)
            def _():
                take(zz)

        return 0

    lax.fori_loop(1, z, take_step, 0)

    def forward_step(i, _):
        zz = z - 1 - i
        with scope("absorb"):
            for yy in range(2):
                arrived_kv(zz, yy, 1 - c)
            absorb(zz)
        return 0

    lax.fori_loop(1, z, forward_step, 0)

    with scope("normalise"):
        attended = (summed[...] / total[...]).astype(BF16)
        log_total = top[...] + jnp.log2(total[...])

    def give(number, block):
        out_stage[number] = block.reshape(2, 128, HEAD_DIM)
        out_copy(number).start()
        out_keep(number).start()

    def out_keep(number):
        return pltpu.make_async_copy(
            out_stage.at[number, y], out_ref.at[number, y], load_sem.at[number]
        )

    def out_copy(number):
        return send(
            out_stage.at[number, 1 - y], out_ref.at[number, y], out_send.at[number],
            out_recv.at[number], beside,
        )

    give(0, attended)

    with scope("own_cot_wait"):
        arrived_c(0, z, 1 - y)
        arrived_c(1, z, y)
    with scope("delta"):
        own_cot = cb[z].reshape(256, HEAD_DIM)
        delta = jnp.sum(own_cot.astype(F32) * attended.astype(F32), axis=1, keepdims=True)
        lane = lax.broadcasted_iota(jnp.int32, (256, 128), 1)
        packed = jnp.where(
            lane == 0, log_total,
            jnp.where(lane == 1, delta, jnp.where(lane == 2, low.astype(F32), high.astype(F32))),
        )
        stats_out[...] = packed.T[:8]

    def st_copy(zz):
        return send(stats_out, stats.at[z], st_send.at[zz], st_recv.at[z], at(zz, y, c))

    def all_stats(do):
        def step(i, _):
            do(st_copy(z - 1 - i))
            return 0

        lax.fori_loop(0, z, step, 0)

    all_stats(start)
    stats[z] = stats_out[...]

    own_keys = keys_of(z)
    own_values = values_of(z)

    def key_side(zz):
        visit = qb[zz].reshape(256, HEAD_DIM)
        visit_cot = cb[zz].reshape(256, HEAD_DIM)
        rest = stats[zz]
        place = z * 512 + lax.broadcasted_iota(jnp.int32, (512, 256), 0)
        seen = (place >= rest[2:3].astype(jnp.int32)) & (place <= rest[3:4].astype(jnp.int32))
        s = jnp.where(seen, visits[zz] * SCALE2, FAR_BELOW)
        p = jnp.exp2(s - rest[0:1])
        slopes = (p * (nt(own_values, visit_cot) - rest[1:2])).astype(BF16)
        return nn(slopes, visit), nn(p.astype(BF16), visit_cot)

    def query_side(zz):
        p = jnp.exp2(scores[zz] - log_total[:, :1])
        slopes = (p * (nt(own_cot, values_of(zz)) - delta)).astype(BF16)
        return nn(slopes, keys_of(zz))

    visits[z] = nt(own_keys, query)
    with scope("key_side_own"):
        dk[...], dv[...] = key_side(z)
    with scope("query_side_own"):
        dq[...] = query_side(z)

    def query_step(i, _):
        with scope("query_side"):
            dq[...] += query_side(z - 1 - i)
        return 0

    lax.fori_loop(0, z, query_step, 0)
    give(1, (dq[...] * SCALE).astype(BF16))

    def arrived_q(zz, yy):
        send(q_own.at[0], qb.at[zz, yy], q_send.at[z, 0], q_recv.at[zz, yy], mate).wait_recv()

    def ahead(zz, _):
        arrived_q(zz, 0)
        arrived_q(zz, 1)
        visits[zz] = nt(own_keys, qb[zz].reshape(256, HEAD_DIM))
        return 0

    lax.fori_loop(z + 1, 4, ahead, 0)

    for copy in tp_first + tp_second:
        copy.wait_send()
    meta_copy().wait_send()
    all_kv(sent)
    earlier(q_copy, sent)
    for part in range(2):
        earlier(functools.partial(c_copy, part), sent)
    all_stats(sent)
    pass_kv(z, 1 - y).wait_send()

    @pl.when(z == 2)
    def _():
        for yy in range(2):
            relay(yy).wait_send()

    def passed(zz, _):
        for yy in range(2):
            pass_kv(zz, yy).wait_send()
        return 0

    lax.fori_loop(0, z, passed, 0)

    def key_step(zz, _):
        with scope("qc_wait"):
            for yy in range(2):
                for part in range(2):
                    arrived_c(part, zz, yy)
        with scope("stats_wait"):
            send(stats_out, stats.at[zz], st_send.at[z], st_recv.at[zz], mate).wait_recv()
        with scope("key_side"):
            more_k, more_v = key_side(zz)
            dk[...] += more_k
            dv[...] += more_v
        return 0

    lax.fori_loop(z + 1, 4, key_step, 0)

    dk4 = dk.reshape(2, 2, 128, HEAD_DIM)
    dv4 = dv.reshape(2, 2, 128, HEAD_DIM)
    with scope("halves"):
        half_out[0] = dk4[:, 1 - c].astype(BF16)
        half_out[1] = dv4[:, 1 - c].astype(BF16)
        half = send(half_out, half_in, half_send, half_recv, mate)
        half.start()
        half.wait_recv()
    with scope("give_kv"):
        give(2, ((dk4[:, c] + half_in[0]) * SCALE).astype(BF16))
        give(3, (dv4[:, c] + half_in[1]).astype(BF16))

    with scope("out_wait"):
        for number in range(4):
            out_keep(number).wait()
            out_copy(number).wait_recv()

    for number in range(4):
        out_copy(number).wait_send()
    half.wait_send()


def spread_kernel(blocks, *refs):
    outs, sem = refs[:4], refs[4]
    copies = [
        pltpu.make_async_copy(
            blocks.at[i, h], outs[i].at[:, pl.ds(h * HEAD_DIM, HEAD_DIM)], sem.at[i, h]
        )
        for i in range(4)
        for h in range(2)
    ]
    for copy in copies:
        copy.start()
    for copy in copies:
        copy.wait()


def on_device(query, key, value, documents, frames, out_cotangent, output_weight):
    hbm = pl.BlockSpec(memory_space=pltpu.HBM)
    vmem = pltpu.VMEM
    dma = pltpu.SemaphoreType.DMA
    depth = out_cotangent.shape[1]
    out = pl.pallas_call(
        kernel,
        name="masked_attention",
        out_shape=pltpu.VMEM((4, 2, 128, HEAD_DIM), BF16),
        in_specs=[hbm] * 7,
        out_specs=pl.BlockSpec(memory_space=vmem),
        scratch_shapes=[
            vmem((256, depth), BF16),
            vmem((depth, 256), BF16),
            vmem((2, 4, 16, depth), BF16),
            vmem((2, 2, 128, 128), BF16),
            vmem((2, 128, 128), BF16),
            vmem((2, 4, 2, 16, 128), BF16),
            vmem((4, 2, 2, 2, 128, 128), BF16),
            vmem((4, 2, 128, 128), BF16),
            vmem((4, 2, 4, 2, 16, 128), BF16),
            vmem((4, 8, 256), F32),
            vmem((8, 256), F32),
            vmem((2, 8, 128), jnp.int32),
            vmem((4, 256, 512), F32),
            vmem((4, 512, 256), F32),
            vmem((256, 128), F32),
            vmem((256, 128), F32),
            vmem((256, 128), F32),
            vmem((256, 128), F32),
            vmem((512, 128), F32),
            vmem((512, 128), F32),
            vmem((2, 2, 128, 128), BF16),
            vmem((2, 2, 128, 128), BF16),
            vmem((4, 2, 128, 128), BF16),
            pltpu.SMEM((1,), jnp.int32), pltpu.SMEM((1,), jnp.int32),
            dma((10,)),
            dma((7,)), dma((7,)),
            dma((4, 2)), dma((4, 2)), dma((2,)), dma((4, 2, 2)),
            dma((4, 2)), dma((4, 2)),
            dma((2, 4, 2)), dma((2, 4, 2)),
            dma((4,)), dma((4,)),
            dma, dma,
            dma, dma,
            dma((4,)), dma((4,)),
        ],
        compiler_params=pltpu.CompilerParams(
            collective_id=0, has_side_effects=True, vmem_limit_bytes=62 * 2**20
        ),
    )(query, key, value, documents, frames, out_cotangent, output_weight)
    return pl.pallas_call(
        spread_kernel,
        name="spread_heads",
        out_shape=[jax.ShapeDtypeStruct((128, 256), BF16)] * 4,
        in_specs=[pl.BlockSpec(memory_space=vmem)],
        out_specs=[hbm] * 4,
        scratch_shapes=[dma((4, 2))],
        compiler_params=pltpu.CompilerParams(vmem_limit_bytes=40 * 2**20),
    )(out)


def solution(mesh):
    whole = P("seq", "tp")
    return jax.shard_map(
        on_device,
        mesh=mesh,
        in_specs=(whole, whole, whole, P("seq"), P("seq"), P(("seq", "tp"), None), P("tp", None)),
        out_specs=(whole, whole, whole, whole),
        check_vma=False,
    )
```
